32 devices in a mesh: ctx: 4 (over y, x), tp: 8 (over z, core).
Axes of the slice: x: 2, y: 2, z: 4, core: 2. Of those that a mesh axis runs over, the one named last changes fastest.
Arguments:
- layer_in: bfloat16 [4096, 2048], P('ctx', 'tp'), may hold values from -6 to 6
- gain_attn: float32 [2048], replicated, may hold values from 0.5 to 1.5
- gain_ffn: float32 [2048], replicated, may hold values from 0.5 to 1.5
- w_query: bfloat16 [2048, 1024], P(None, 'tp'), may hold values from -0.1875 to 0.1875
- w_key: bfloat16 [2048, 1024], P(None, 'tp'), may hold values from -0.1875 to 0.1875
- w_value: bfloat16 [2048, 1024], P(None, 'tp'), may hold values from -0.125 to 0.125
- w_out: bfloat16 [1024, 2048], P('tp'), may hold values from -1.5 to 1.5
- w_gate: bfloat16 [2048, 4096], P(None, 'tp'), may hold values from -0.125 to 0.125
- w_up: bfloat16 [2048, 4096], P(None, 'tp'), may hold values from -0.125 to 0.125
- w_down: bfloat16 [4096, 2048], P('tp'), may hold values from -0.09375 to 0.09375
- doc_ids: int32 [4096], P('ctx'), may hold values from 0 to 3, as said below
- positions: int32 [4096], P('ctx'), may hold values from 0 to 3071, as said below
- cotangent: bfloat16 [4096, 2048], P('ctx', 'tp'), may hold values from -6 to 6
Outputs:
- out: bfloat16 [4096, 2048], P('ctx', 'tp')
- grad_input: float32 [4096, 2048], P('ctx', 'tp')
- grad_gain_attn: float32 [2048], P('tp')
- grad_gain_ffn: float32 [2048], P('tp')
- grad_query: float32 [2048, 1024], P(None, 'tp')
- grad_key: float32 [2048, 1024], P(None, 'tp')
- grad_value: float32 [2048, 1024], P(None, 'tp')
- grad_out: float32 [1024, 2048], P('tp')
- grad_gate: float32 [2048, 4096], P(None, 'tp')
- grad_up: float32 [2048, 4096], P(None, 'tp')
- grad_down: float32 [4096, 2048], P('tp')
The draws below stay inside these ranges and needn't reach their ends.
Inputs may be any that keep to these rules, and one draw needn't show every extreme that they name: `doc_ids`: never falls along the sequence; four documents, starting at 0. `positions`: 0 at a document's first token and rising by one within the document.
All inputs are finite; a program needn't handle non-finite values.
Results may differ from the reference program's by a relative error of at most 0.013.
The reference program's roundings to bfloat16 on the way count: a program that leaves them out, or rounds other values in their place, can miss the bound.
Values may be sent and summed in bfloat16 or wider, within the bound.
No kernel may reach another device: no remote copies, remote signals or barrier semaphores. Data moves between devices by JAX's collectives and lax.ppermute only.
A program may use at most 192 MiB of HBM per device.

```python
import math
import jax
import jax.numpy as jnp
from jax import lax

D = 2048
HDIM = 128
HEAD_DEV = 1
TOK_DEV = 1024
HEADS = 8
FF = 4096
LENGTH = 4096
N_TP = 8


def doc_layout(key):
    token_index = jnp.arange(LENGTH, dtype=jnp.int32)
    half_group = max(TOK_DEV // 2, 1)
    first_key, cut_key = jax.random.split(key, 2)
    first = jax.random.randint(first_key, (), 1, half_group + 1)
    last = first + LENGTH - TOK_DEV
    cut = last + jax.random.randint(cut_key, (), 1, TOK_DEV - first)
    starts = (token_index == 0) | (token_index == first) | (token_index == last) | (token_index == cut)
    numbers = jnp.cumsum(starts.astype(jnp.int32)) - 1
    begins = lax.cummax(jnp.where(starts, token_index, 0), axis=0)
    return (numbers.astype(jnp.int32), (token_index - begins).astype(jnp.int32))


def draw_doc_ids(key, part):
    numbers, places = doc_layout(key)
    return numbers


def draw_positions(key, part):
    numbers, places = doc_layout(key)
    return places


def block_scale(key, dims, cuts, smallest, high):
    level, own = 1.0, jax.random.fold_in(key, 6)
    for axis_at, parts in cuts:
        steps = jnp.exp(jax.random.uniform(jax.random.fold_in(own, axis_at), (parts,), jnp.float32, smallest / len(cuts), high / len(cuts)))
        level = level * jnp.repeat(steps, dims[axis_at] // parts).reshape([-1 if axis == axis_at else 1 for axis in range(len(dims))])
    return level


def centred(stream_key, shape, spread, most, cuts=(), kind=jnp.bfloat16):
    factor_of = block_scale(stream_key, shape, cuts, -0.22, 0.18) if cuts else 1.0
    values = jax.random.normal(stream_key, shape, jnp.float32) * spread * factor_of
    return jnp.minimum(jnp.maximum(values, -most), most).astype(kind)


def setup_inputs(seed: int = 0) -> dict:
    key_of = jax.random.split(jax.random.key(seed), 14)
    layer_in = centred(key_of[0], (LENGTH, D), 1.0, 6.0, ((0, 4), (1, 8)))
    gain_attn = jnp.clip(1.0 + 0.1 * jax.random.normal(key_of[1], (D,), jnp.float32), 0.5, 1.5)
    gain_ffn = jnp.clip(1.0 + 0.1 * jax.random.normal(key_of[2], (D,), jnp.float32), 0.5, 1.5)
    w_query = centred(key_of[3], (D, HEADS * HDIM), (D // 2) ** -0.5, 0.1875, ((1, 8),))
    w_key = centred(key_of[4], (D, HEADS * HDIM), (D // 2) ** -0.5, 0.1875, ((1, 8),))
    w_value = centred(key_of[5], (D, HEADS * HDIM), D ** -0.5, 0.125, ((1, 8),))
    w_out = centred(key_of[6], (HEADS * HDIM, D), 16 ** -0.5, 1.5, ((0, 8),))
    w_gate = centred(key_of[7], (D, FF), D ** -0.5, 0.125, ((1, 8),))
    w_up = centred(key_of[8], (D, FF), D ** -0.5, 0.125, ((1, 8),))
    w_down = centred(key_of[9], (FF, D), FF ** -0.5, 0.09375, ((0, 8),))
    doc_ids = draw_doc_ids(jax.random.fold_in(key_of[13], 71), 0)
    positions = draw_positions(jax.random.fold_in(key_of[13], 71), 0)
    cotangent = centred(key_of[12], (LENGTH, D), 1.0, 6.0, ((0, 4), (1, 8)))
    return {"layer_in": layer_in, "gain_attn": gain_attn, "gain_ffn": gain_ffn, "w_query": w_query, "w_key": w_key, "w_value": w_value, "w_out": w_out, "w_gate": w_gate, "w_up": w_up, "w_down": w_down, "doc_ids": doc_ids, "positions": positions, "cotangent": cotangent}


EPS = 1e-05
THETA = 10000.0

@jax.custom_vjp
def low(v):
    return lax.optimization_barrier(v.astype(jnp.bfloat16)).astype(jnp.float32)

@jax.custom_vjp
def low_back(v):
    return v

def low_keep(v):
    return (low(v), None)

def low_pass(kept, grad):
    return (grad,)

def back_keep(v):
    return (v, None)

def back_low(kept, grad):
    return (low(grad),)
low.defvjp(low_keep, low_pass)
low_back.defvjp(back_keep, back_low)

def matmul(left, right):
    return jnp.dot(left, right, precision=lax.Precision.HIGHEST)

def rms_norm(values, gain):
    return values * lax.rsqrt(lax.optimization_barrier(jnp.mean(values * values, axis=-1, keepdims=True)) + EPS) * gain

def rope_tables(places, width):
    half_width = width // 2
    freq = THETA ** (-(jnp.arange(half_width, dtype=jnp.float32) * 2.0 / width))
    angle = places.astype(jnp.float32)[:, None] * freq[None, :]
    return (jnp.cos(angle)[:, None, :], jnp.sin(angle)[:, None, :])

def rotate(values, cosine, sine_table):
    half_width = values.shape[-1] // 2
    first = values[..., :half_width]
    second = values[..., half_width:]
    return jnp.concatenate([first * cosine - second * sine_table, first * sine_table + second * cosine], axis=-1)

def reference(layer_in, gain_attn, gain_ffn, w_query, w_key, w_value, w_out, w_gate, w_up, w_down, doc_ids, positions, cotangent):
    heads = HEAD_DEV * N_TP
    score_scale = 1.0 / math.sqrt(HDIM)
    score_bias = -math.log(LENGTH)
    q_span = math.gcd(LENGTH, 512)
    blocks = LENGTH // q_span
    cosine, sine_table = rope_tables(positions, HDIM)
    token_index = jnp.arange(LENGTH, dtype=jnp.int32)

    def attend(q_rot, k_rot, values):

        def one_block(pieces):
            query_block, doc_block, index_block = pieces
            scores = jnp.einsum('qhd,khd->hqk', query_block, k_rot, precision=lax.Precision.HIGHEST) * score_scale + score_bias
            scores = low_back(scores)
            visible = (doc_block[:, None] == doc_ids[None, :]) & (token_index[None, :] <= index_block[:, None])
            weights = jnp.where(visible[None], low(jax.nn.sigmoid(scores)), 0.0)
            mixed = jnp.einsum('hqk,khd->qhd', weights, values, precision=lax.Precision.HIGHEST)
            return low(low_back(mixed)).reshape(q_span, heads * HDIM)
        result = lax.map(jax.checkpoint(one_block), (q_rot.reshape(blocks, q_span, heads, HDIM), doc_ids.reshape(blocks, q_span), token_index.reshape(blocks, q_span)))
        return result.reshape(LENGTH, heads * HDIM)

    def forward(layer_x, gain_one, gain_two, query_w, key_w, value_w, out_w, gate_w, up_w, down_w):
        normed = low(rms_norm(layer_x, gain_one))
        q_pre = low_back(matmul(normed, query_w)).reshape(LENGTH, heads, HDIM)
        k_pre = low_back(matmul(normed, key_w)).reshape(LENGTH, heads, HDIM)
        values = low(low_back(matmul(normed, value_w))).reshape(LENGTH, heads, HDIM)
        q_rot = low(rotate(q_pre, cosine, sine_table))
        k_rot = low(rotate(k_pre, cosine, sine_table))
        mixed = attend(q_rot, k_rot, values)
        middle = layer_x + low_back(matmul(mixed, out_w))
        normed_two = low(rms_norm(middle, gain_two))
        gate_pre = low_back(matmul(normed_two, gate_w))
        up_proj = low_back(matmul(normed_two, up_w))
        hidden = low(jax.nn.silu(gate_pre) * up_proj)
        return middle + low_back(matmul(hidden, down_w))
    inputs = (layer_in.astype(jnp.float32), gain_attn.astype(jnp.float32), gain_ffn.astype(jnp.float32), w_query.astype(jnp.float32), w_key.astype(jnp.float32), w_value.astype(jnp.float32), w_out.astype(jnp.float32), w_gate.astype(jnp.float32), w_up.astype(jnp.float32), w_down.astype(jnp.float32))
    result, pullback = jax.vjp(forward, *inputs)
    grads = pullback(cotangent.astype(jnp.float32))
    return (result.astype(jnp.bfloat16), grads[0], grads[1], grads[2], grads[3], grads[4], grads[5], grads[6], grads[7], grads[8], grads[9])
```

```python
import math

import jax
import jax.numpy as jnp
from jax import lax
from jax.sharding import PartitionSpec as P

HDIM = 128
EPS = 1e-05
THETA = 10000.0
BF = jnp.bfloat16
F32 = jnp.float32


def rope_tables(places, width):
    half_width = width // 2
    freq = THETA ** (-(jnp.arange(half_width, dtype=F32) * 2.0 / width))
    angle = places.astype(F32)[:, None] * freq[None, :]
    return jnp.cos(angle), jnp.sin(angle)


def rotate(values, cosine, sine):
    half = values.shape[-1] // 2
    first, second = values[..., :half], values[..., half:]
    return jnp.concatenate([first * cosine - second * sine, first * sine + second * cosine], axis=-1)


def rotate_back(values, cosine, sine):
    half = values.shape[-1] // 2
    first, second = values[..., :half], values[..., half:]
    return jnp.concatenate([first * cosine + second * sine, second * cosine - first * sine], axis=-1)


def dot(a, b, dims, out=F32):
    return lax.dot_general(a, b, (dims, ((), ())), preferred_element_type=F32).astype(out)


NN = ((1,), (0,))
NT = ((1,), (1,))
TN = ((0,), (0,))


def folded(n):
    return [0] + list(range(1, n, 2)) + list(range(n - 2 + n % 2, 0, -2))


class Tp:
    def __init__(self, n_tp):
        self.n = n_tp
        self.pairs = n_tp // 2
        self.ring = folded(self.pairs)
        place = [self.ring.index(z) for z in range(self.pairs)]
        self.core_perm = [(i, i ^ 1) for i in range(n_tp)]
        self.ring_perm = []
        for i in range(n_tp):
            z, c = divmod(i, 2)
            self.ring_perm.append((i, self.ring[(place[z] + 1) % self.pairs] * 2 + c))
        order, where = [], []
        for i in range(n_tp):
            z, c = divmod(i, 2)
            row = []
            for j in range(self.pairs):
                src = self.ring[(place[z] - j) % self.pairs]
                row += [src * 2 + c, src * 2 + 1 - c]
            order.append(row)
            where.append([row.index(b) for b in range(n_tp)])
        me = lax.axis_index("tp")
        self.order = [jnp.asarray([order[i][k] for i in range(n_tp)], jnp.int32)[me] for k in range(n_tp)]
        self.where = [jnp.asarray([where[i][k] for i in range(n_tp)], jnp.int32)[me] for k in range(n_tp)]

    def core(self, a):
        return lax.ppermute(a, "tp", self.core_perm)

    def step(self, a):
        return lax.ppermute(a, "tp", self.ring_perm)

    def gather(self, block):
        got, cur = [], block
        for j in range(self.pairs):
            if j:
                cur = self.step(cur)
            got += [cur, self.core(cur)]
        return got

    def scatter(self, partial):
        share = partial.shape[1] // self.n
        acc = None
        for j in list(range(1, self.pairs)) + [0]:
            own = partial[:, 2 * j * share : (2 * j + 1) * share].astype(F32)
            other = self.core(partial[:, (2 * j + 1) * share : (2 * j + 2) * share])
            term = own + other.astype(F32)
            if acc is not None:
                term = term + self.step(acc.astype(BF)).astype(F32)
            acc = term
        return acc

    def total(self, small):
        out = small + self.core(small)
        cur, acc = out, out
        for _ in range(1, self.pairs):
            cur = self.step(cur)
            acc = acc + cur
        return acc

    def to_ring(self, a, axis):
        size = a.shape[axis] // self.n
        return jnp.concatenate(
            [lax.dynamic_slice_in_dim(a, k * size, size, axis) for k in self.order], axis=axis
        )

    def from_ring(self, a, axis):
        size = a.shape[axis] // self.n
        return jnp.concatenate(
            [lax.dynamic_slice_in_dim(a, k * size, size, axis) for k in self.where], axis=axis
        )


def per_device(
    layer_in,
    gain_attn,
    gain_ffn,
    w_query,
    w_key,
    w_value,
    w_out,
    w_gate,
    w_up,
    w_down,
    doc_ids,
    positions,
    cotangent,
):
    tok, share = layer_in.shape
    n_ctx, n_tp = lax.axis_size("ctx"), lax.axis_size("tp")
    width = share * n_tp
    heads = w_query.shape[1] // HDIM
    head_width = heads * HDIM
    hid = w_gate.shape[1]
    tp = Tp(n_tp)
    rank = lax.axis_index("ctx")
    own = lax.axis_index("tp") * share
    seq_len = tok * n_ctx
    score_scale = 1.0 / math.sqrt(HDIM)
    score_bias = -math.log(seq_len)
    span = math.gcd(tok, 512)

    gain_a_own = lax.dynamic_slice_in_dim(gain_attn, own, share, 0)
    gain_f_own = lax.dynamic_slice_in_dim(gain_ffn, own, share, 0)
    gain_a = tp.to_ring(gain_attn, 0)
    gain_f = tp.to_ring(gain_ffn, 0)
    wqkv = tp.to_ring(jnp.concatenate([w_query, w_key, w_value], axis=1), 0)
    wo = tp.to_ring(w_out, 1)
    wgu = tp.to_ring(jnp.concatenate([w_gate, w_up], axis=1), 0)
    wd = tp.to_ring(w_down, 1)

    x_full = jnp.concatenate(tp.gather(layer_in), axis=1)
    x_wide = x_full.astype(F32)
    r1 = lax.rsqrt(jnp.mean(x_wide * x_wide, axis=-1, keepdims=True) + EPS)
    normed = (x_wide * r1 * gain_a).astype(BF)
    qkv = dot(normed, wqkv, NN)
    q_pre, k_pre, v_pre = jnp.split(qkv, 3, axis=1)
    cosine, sine = rope_tables(positions, HDIM)
    cosine, sine = cosine[:, None, :], sine[:, None, :]
    q_rot = rotate(q_pre.reshape(tok, heads, HDIM), cosine, sine).astype(BF)
    k_rot = rotate(k_pre.reshape(tok, heads, HDIM), cosine, sine).astype(BF)
    values = v_pre.astype(BF)
    kv_own = jnp.concatenate([k_rot.reshape(tok, head_width), values], axis=1)

    def shift(a, s):
        return lax.ppermute(a, "ctx", [(r, r + s) for r in range(n_ctx) if 0 <= r + s < n_ctx])

    kv_all = jnp.concatenate([shift(kv_own, s) for s in range(n_ctx - 1, 0, -1)] + [kv_own], axis=0)
    base = (rank - (n_ctx - 1)) * tok
    q_index = rank * tok + jnp.arange(tok, dtype=jnp.int32)
    q_start = q_index - positions
    first = jnp.maximum((q_start[0] - base) // span, 0)
    last = seq_len // span

    def scores_block(b):
        kv = lax.dynamic_slice_in_dim(kv_all, b * span, span, 0)
        keys = kv[:, :head_width].reshape(span, heads, HDIM)
        vals = kv[:, head_width:].reshape(span, heads, HDIM)
        s = jnp.einsum("qhd,khd->hqk", q_rot, keys, preferred_element_type=F32)
        s = s * score_scale + score_bias
        k_index = base + b * span + jnp.arange(span, dtype=jnp.int32)
        visible = (k_index[None, :] >= q_start[:, None]) & (k_index[None, :] <= q_index[:, None])
        return keys, vals, visible[None], jax.nn.sigmoid(s)

    def forward_step(b, total):
        keys, vals, visible, sig = scores_block(b)
        weights = jnp.where(visible, sig, 0.0).astype(BF)
        return total + jnp.einsum("hqk,khd->qhd", weights, vals, preferred_element_type=F32)

    mixed = lax.fori_loop(first, last, forward_step, jnp.zeros((tok, heads, HDIM), F32))
    mixed = mixed.reshape(tok, head_width).astype(BF)

    h = layer_in.astype(F32) + tp.scatter(dot(mixed, wo, NN, BF))

    cot_full = jnp.concatenate(tp.gather(cotangent), axis=1)
    hg_full = jnp.concatenate(tp.gather((h * gain_f_own).astype(BF)), axis=1)
    h_wide = hg_full.astype(F32) * (1.0 / gain_f)
    r2 = lax.rsqrt(jnp.mean(h_wide * h_wide, axis=-1, keepdims=True) + EPS)
    pre = dot(hg_full, wgu, NN) * r2
    gate, up = pre[:, :hid], pre[:, hid:]
    sig = jax.nn.sigmoid(gate)
    silu = gate * sig
    hidden = (silu * up).astype(BF)
    g_hidden = dot(cot_full, wd, NT)
    g_gate = g_hidden * up * sig * (1.0 + gate * (1.0 - sig))
    g_up = g_hidden * silu
    m2 = tp.total(jnp.sum(g_gate * gate + g_up * up, axis=-1)) / width
    ggu = (jnp.concatenate([g_gate, g_up], axis=1) * r2).astype(BF)
    dn2 = tp.scatter(dot(ggu, wgu, NT, BF))
    grad_down = dot(hidden, cot_full, TN, BF)
    grad_gu = dot(hg_full, ggu, TN, BF)
    g_h = cotangent.astype(F32) + gain_f_own * dn2 - (r2 * r2 * m2[:, None]) * h
    grad_gain_two = jnp.sum(dn2 * h, axis=0)
    out = h + tp.scatter(dot(hidden, wd, NN, BF))

    g_hb = jnp.concatenate(tp.gather(g_h.astype(BF)), axis=1)
    grad_out = dot(mixed, g_hb, TN, BF)
    g_mixed = dot(g_hb, wo, NT, BF).reshape(tok, heads, HDIM)

    def backward_step(b, state):
        g_query_sum, g_kv = state
        keys, vals, visible, sig = scores_block(b)
        weights = jnp.where(visible, sig, 0.0).astype(BF)
        g_values = jnp.einsum("hqk,qhd->khd", weights, g_mixed, preferred_element_type=F32)
        g_weights = jnp.einsum("qhd,khd->hqk", g_mixed, vals, preferred_element_type=F32)
        g_scores = jnp.where(visible, g_weights * sig * (1.0 - sig), 0.0).astype(BF)
        g_query_sum = g_query_sum + jnp.einsum("hqk,khd->qhd", g_scores, keys, preferred_element_type=F32)
        g_keys = jnp.einsum("hqk,qhd->khd", g_scores, q_rot, preferred_element_type=F32)
        g_block = jnp.concatenate(
            [g_keys.reshape(span, head_width) * score_scale, g_values.reshape(span, head_width)], axis=1
        )
        return g_query_sum, lax.dynamic_update_slice_in_dim(g_kv, g_block, b * span, 0)

    g_query, g_kv_all = lax.fori_loop(
        first,
        last,
        backward_step,
        (jnp.zeros((tok, heads, HDIM), F32), jnp.zeros((seq_len, 2 * head_width), F32)),
    )
    g_kv = g_kv_all[-tok:]
    for s in range(n_ctx - 1, 0, -1):
        at = (n_ctx - 1 - s) * tok
        g_kv = g_kv + shift(g_kv_all[at : at + tok].astype(BF), -s).astype(F32)
    g_query = rotate_back(g_query * score_scale, cosine, sine).reshape(tok, head_width)
    g_key = rotate_back(g_kv[:, :head_width].reshape(tok, heads, HDIM), cosine, sine).reshape(tok, head_width)
    g_qkv = jnp.concatenate([g_query, g_key, g_kv[:, head_width:]], axis=1)
    m1 = tp.total(jnp.sum(g_qkv * qkv, axis=-1)) / width
    g_qkv = g_qkv.astype(BF)
    grad_qkv = dot(normed, g_qkv, TN, BF)
    dn1 = tp.scatter(dot(g_qkv, wqkv, NT, BF))
    x_own = layer_in.astype(F32)
    x_hat = x_own * r1
    g_input = g_h + r1 * (dn1 * gain_a_own - x_hat * m1[:, None])
    grad_gain_one = jnp.sum(dn1 * x_hat, axis=0)

    grad_down, grad_gu = lax.psum((grad_down, grad_gu), "ctx")
    grad_out, grad_qkv = lax.psum((grad_out, grad_qkv), "ctx")
    gains = lax.psum(jnp.concatenate([grad_gain_one, grad_gain_two]), "ctx")
    grad_qkv = tp.from_ring(grad_qkv, 0).astype(F32)
    grad_gu = tp.from_ring(grad_gu, 0).astype(F32)
    return (
        out.astype(BF),
        g_input,
        gains[:share],
        gains[share:],
        grad_qkv[:, :head_width],
        grad_qkv[:, head_width : 2 * head_width],
        grad_qkv[:, 2 * head_width :],
        tp.from_ring(grad_out, 1).astype(F32),
        grad_gu[:, :hid],
        grad_gu[:, hid:],
        tp.from_ring(grad_down, 1).astype(F32),
    )


def solution(mesh):
    row, col = P("tp", None), P(None, "tp")
    both = P("ctx", "tp")
    in_specs = (both, P(), P(), col, col, col, row, col, col, row, P("ctx"), P("ctx"), both)
    out_specs = (both, both, P("tp"), P("tp"), col, col, col, row, col, col, row)
    return jax.shard_map(
        per_device, mesh=mesh, in_specs=in_specs, out_specs=out_specs, check_vma=False
    )
```

```python
import functools
import math

import jax
import jax.numpy as jnp
from jax import lax
from jax.experimental import pallas as pl
from jax.experimental.pallas import tpu as pltpu
from jax.sharding import PartitionSpec as P

HDIM = 128
EPS = 1e-05
THETA = 10000.0
LOG2E = math.log2(math.e)
SCALE = 1.0 / math.sqrt(HDIM)
BF = jnp.bfloat16
F32 = jnp.float32
I32 = jnp.int32
BQ, BK = 512, 512
VMEM_BYTES = 60 * 1024 * 1024
CHUNKS = 1
COST = 1.0

SM = pl.BlockSpec(memory_space=pltpu.SMEM)
VM = pl.BlockSpec(memory_space=pltpu.VMEM)


def shape(dims, dtype):
    return jax.ShapeDtypeStruct(dims, dtype)


def params():
    return pltpu.CompilerParams(vmem_limit_bytes=VMEM_BYTES)


def cost(mults, size):
    return pl.CostEstimate(flops=int(2 * mults * COST), bytes_accessed=int(size * COST), transcendentals=0)


def nn(a, b):
    return lax.dot_general(a, b, (((1,), (0,)), ((), ())), preferred_element_type=F32)


def nt(a, b):
    return lax.dot_general(a, b, (((1,), (1,)), ((), ())), preferred_element_type=F32)


def tn(a, b):
    return lax.dot_general(a, b, (((0,), (0,)), ((), ())), preferred_element_type=F32)


def add(a, b):
    return b if a is None else a + b


def tiles(width, k, n=None):
    return pl.ds(pl.multiple_of(k * width, width), width)


def row_sums(a):
    high = a.astype(BF)
    low = (a - high.astype(F32)).astype(BF)
    ones = jnp.ones((8, a.shape[1]), BF)
    return nt(ones, high) + nt(ones, low)


def qkv_kernel(n, order, *refs):
    xs = refs[:n]
    gain, wq, wk, wv, cos, sin, normed, q, kv, r1_out = refs[n:]
    share = xs[0].shape[1]
    squares = None
    for k in range(n):
        v = xs[k][...].astype(F32)
        squares = add(squares, v * v)
    r1 = lax.rsqrt(jnp.sum(squares, axis=-1, keepdims=True) / (n * share) + EPS)
    sums = [None] * 3
    for k in range(n):
        block = (xs[k][...].astype(F32) * r1 * gain[pl.ds(order[k], 1), :]).astype(BF)
        normed[:, k * share : (k + 1) * share] = block
        rows = tiles(share, order[k])
        for i, w in enumerate((wq, wk, wv)):
            sums[i] = add(sums[i], nn(block, w[rows, :]))
    c, s = cos[...], sin[...]

    def rotated(v):
        return v * c + pltpu.roll(v, HDIM // 2, 1) * s

    q[...] = rotated(sums[0]).astype(BF)
    kv[:, :HDIM] = rotated(sums[1]).astype(BF)
    kv[:, HDIM:] = sums[2].astype(BF)
    r1_out[...] = jnp.broadcast_to(r1, r1_out.shape)


def call_qkv(order, xs, gain, wq, wk, wv, cos, sin):
    n = len(xs)
    tok, share = xs[0].shape
    bt = min(tok, 256)

    def row(w):
        return pl.BlockSpec((bt, w), lambda i, o: (i, 0))

    def full(a):
        return pl.BlockSpec(a.shape, lambda i, o: (0, 0))

    spec = pltpu.PrefetchScalarGridSpec(
        num_scalar_prefetch=1,
        grid=(tok // bt,),
        in_specs=[row(share)] * n + [full(a) for a in (gain, wq, wk, wv)] + [row(HDIM)] * 2,
        out_specs=[row(n * share), row(HDIM), row(2 * HDIM), row(128)],
    )
    return pl.pallas_call(
        functools.partial(qkv_kernel, n),
        grid_spec=spec,
        out_shape=[
            shape((tok, n * share), BF),
            shape((tok, HDIM), BF),
            shape((tok, 2 * HDIM), BF),
            shape((tok, 128), F32),
        ],
        compiler_params=params(),
        cost_estimate=cost(5 * tok * n * share * HDIM * 4, 10 * tok * n * share),
        name="norm_qkv",
    )(order, *xs, gain, wq, wk, wv, cos, sin)


def edges_of(rank, tok, starts):
    t = starts.reshape(tok // BQ, BQ)
    return jnp.concatenate([(rank * tok)[None], jnp.stack([t[:, 0], t[:, -1]], axis=1).reshape(-1)])


def sigmoid_of(raw, bias):
    return 1.0 / (1.0 + jnp.exp2(raw * (-LOG2E * SCALE) - bias * LOG2E))


def own_kernel(bias, tok, edges, start, q, kv, total):
    base = edges[0]
    for qi in range(tok // BQ):
        rows = slice(qi * BQ, (qi + 1) * BQ)
        q_tile = q[rows, :]
        first_key = start[rows, :] - base
        q_index = qi * BQ + lax.broadcasted_iota(I32, (BQ, 1), 0)

        def body(ki, acc):
            at = tiles(BK, ki)
            w = sigmoid_of(nt(q_tile, kv[at, :HDIM]), bias)
            k_index = ki * BK + lax.broadcasted_iota(I32, (BQ, BK), 1)
            w = jnp.where((k_index >= first_key) & (k_index <= q_index), w, 0.0)
            return acc + nn(w.astype(BF), kv[at, HDIM:])

        low = jnp.maximum(edges[1 + 2 * qi] - base, 0) // BK
        high = ((qi + 1) * BQ + BK - 1) // BK
        total[rows, :] = lax.fori_loop(low, high, body, jnp.zeros((BQ, HDIM), F32))


def far_kernel(bias, tok, q0, n_far, n, edges, order, start, q, acc, wo, *refs):
    kvs, mixed, pieces = refs[:n_far], refs[n_far], refs[n_far + 1 :]
    share = wo.shape[1] // n
    n_keys = tok // BK
    for qi in range(q.shape[0] // BQ):
        rows = slice(qi * BQ, (qi + 1) * BQ)
        at_first, at_last = 1 + 2 * (q0 // BQ + qi), 2 + 2 * (q0 // BQ + qi)
        q_tile = q[rows, :]
        total = acc[rows, :]
        for i in range(n_far):
            base = edges[0] - (i + 1) * tok
            kv = kvs[i]
            first_key = start[rows, :] - base

            def body(ki, total, masked):
                at = tiles(BK, ki)
                w = sigmoid_of(nt(q_tile, kv[at, :HDIM]), bias)
                if masked:
                    k_index = ki * BK + lax.broadcasted_iota(I32, (BQ, BK), 1)
                    w = jnp.where(k_index >= first_key, w, 0.0)
                return total + nn(w.astype(BF), kv[at, HDIM:])

            low = jnp.clip(edges[at_first] - base, 0, tok) // BK
            mid = jnp.clip(edges[at_last] - base + BK - 1, 0, tok) // BK
            mid = jnp.maximum(low, mid)
            total = lax.fori_loop(low, mid, functools.partial(body, masked=True), total)
            total = lax.fori_loop(mid, n_keys, functools.partial(body, masked=False), total)
        rounded = total.astype(BF)
        mixed[rows, :] = rounded
        for k in range(n):
            pieces[k][rows, :] = nn(rounded, wo[:, tiles(share, order[k])]).astype(BF)


def tile_back(bias, q_tile, g_tile, k_tile, v_tile, keep, g_query, rows, sums):
    s = sigmoid_of(nt(k_tile, q_tile), bias)
    g_weight = nt(v_tile, g_tile)
    if keep is not None:
        s = jnp.where(keep, s, 0.0)
    g_s = (g_weight * (s * (1.0 - s))).astype(BF)
    g_value = sums[1] + nn(s.astype(BF), g_tile)
    g_key = sums[0] + nn(g_s, q_tile)
    g_query[rows, :] = g_query[rows, :] + tn(g_s, k_tile)
    return g_key, g_value


def count_tiles(edges, n_q, which, limit):
    return sum([(edges[which + 2 * i] <= limit).astype(I32) for i in range(n_q)], jnp.int32(0))


def far_back_kernel(bias, tok, n_far, edges, start, q, g, *refs):
    kvs, g_query, outs = refs[:n_far], refs[n_far], refs[n_far + 1 :]
    n_q = tok // BQ
    g_query[...] = jnp.zeros_like(g_query)
    for i in reversed(range(n_far)):
        base = edges[0] - (i + 1) * tok
        kv, out = kvs[i], outs[i]

        def key_tile(ki, carry):
            at = tiles(BK, ki)
            k_tile, v_tile = kv[at, :HDIM], kv[at, HDIM:]
            key0 = base + ki * BK
            high = count_tiles(edges, n_q, 1, key0 + BK - 1)
            mid = count_tiles(edges, n_q, 2, key0)

            def body(qi, sums, masked):
                r = tiles(BQ, qi)
                keep = None
                if masked:
                    keep = key0 + lax.broadcasted_iota(I32, (BK, BQ), 0) >= start[:, r]
                return tile_back(bias, q[r, :], g[r, :], k_tile, v_tile, keep, g_query, r, sums)

            zero = jnp.zeros((BK, HDIM), F32)
            sums = lax.fori_loop(0, mid, functools.partial(body, masked=False), (zero, zero))
            g_key, g_value = lax.fori_loop(mid, high, functools.partial(body, masked=True), sums)
            out[at, :HDIM] = (g_key * SCALE).astype(BF)
            out[at, HDIM:] = g_value.astype(BF)
            return carry

        live = jnp.logical_and(base >= 0, edges[1] <= base + tok - 1)

        @pl.when(live)
        def _():
            lax.fori_loop(0, tok // BK, key_tile, 0)

        @pl.when(jnp.logical_not(live))
        def _():
            out[...] = jnp.zeros_like(out)


def own_back_kernel(bias, tok, edges, start, q, g, kv, g_query_in, g_query, out):
    n_q = tok // BQ
    base = edges[0]
    g_query[...] = g_query_in[...]
    for ki in range(tok // BK):
        at = slice(ki * BK, (ki + 1) * BK)
        k_tile, v_tile = kv[at, :HDIM], kv[at, HDIM:]
        key0 = base + ki * BK

        def body(qi, sums):
            r = tiles(BQ, qi)
            k_index = key0 + lax.broadcasted_iota(I32, (BK, BQ), 0)
            q_index = base + qi * BQ + lax.broadcasted_iota(I32, (1, BQ), 1)
            keep = (k_index >= start[:, r]) & (k_index <= q_index)
            return tile_back(bias, q[r, :], g[r, :], k_tile, v_tile, keep, g_query, r, sums)

        zero = jnp.zeros((BK, HDIM), F32)
        high = count_tiles(edges, n_q, 1, key0 + BK - 1)
        g_key, g_value = lax.fori_loop((ki * BK) // BQ, high, body, (zero, zero))
        out[at, :HDIM] = g_key * SCALE
        out[at, HDIM:] = g_value


def call_own(bias, edges, start, q, kv):
    tok = q.shape[0]
    return pl.pallas_call(
        functools.partial(own_kernel, bias, tok),
        out_shape=shape((tok, HDIM), F32),
        in_specs=[SM, VM, VM, VM],
        out_specs=VM,
        compiler_params=params(),
        cost_estimate=cost(16 * tok * tok * HDIM, 4 * tok * HDIM),
        name="attend_own",
    )(edges, start, q, kv)


def call_far(bias, tok, c, rows, edges, order, start, q, acc, wo, kvs):
    n = order.shape[0]

    def part(w):
        return pl.BlockSpec((rows, w), lambda i: (c, 0))

    def full(a):
        return pl.BlockSpec(a.shape, lambda i: (0, 0))

    out = pl.BlockSpec((rows, HDIM), lambda i: (0, 0))
    share = wo.shape[1] // n
    return pl.pallas_call(
        functools.partial(far_kernel, bias, tok, c * rows, len(kvs), n),
        grid=(1,),
        out_shape=[shape((rows, HDIM), BF)] + [shape((rows, share), BF)] * n,
        in_specs=[SM, SM, part(1), part(HDIM), part(HDIM), full(wo)] + [full(a) for a in kvs],
        out_specs=[out] + [pl.BlockSpec((rows, share), lambda i: (0, 0))] * n,
        compiler_params=params(),
        cost_estimate=cost(20 * rows * tok * HDIM + 12 * rows * n * share * HDIM, 4 * rows * n * share),
        name="attend_far",
    )(edges, order, start, q, acc, wo, *kvs)


def call_far_back(bias, edges, start, q, g, kvs):
    tok = q.shape[0]
    return pl.pallas_call(
        functools.partial(far_back_kernel, bias, tok, len(kvs)),
        out_shape=[shape((tok, HDIM), F32)] + [shape((tok, 2 * HDIM), BF)] * len(kvs),
        in_specs=[SM] + [VM] * (3 + len(kvs)),
        out_specs=[VM] * (1 + len(kvs)),
        compiler_params=params(),
        cost_estimate=cost(48 * tok * tok * HDIM, 16 * tok * HDIM),
        name="attend_far_back",
    )(edges, start, q, g, *kvs)


def call_own_back(bias, edges, start, q, g, kv, g_query):
    tok = q.shape[0]
    return pl.pallas_call(
        functools.partial(own_back_kernel, bias, tok),
        out_shape=[shape((tok, HDIM), F32), shape((tok, 2 * HDIM), F32)],
        in_specs=[SM] + [VM] * 5,
        out_specs=[VM] * 2,
        compiler_params=params(),
        cost_estimate=cost(28 * tok * tok * HDIM, 16 * tok * HDIM),
        name="attend_own_back",
    )(edges, start, q, g, kv, g_query)


def ffn_kernel(n, order, *refs):
    hs = refs[:n]
    cot, inv_gain, wg, wu, wd, hidden, g_gu, r2_out, m2 = refs[n : n + 9]
    pieces = refs[n + 9 :]
    share, hid = hs[0].shape[1], wg.shape[1]
    squares = gate = up = None
    for k in range(n):
        h = hs[k][...]
        v = h.astype(F32) * inv_gain[pl.ds(order[k], 1), :]
        squares = add(squares, v * v)
        rows = tiles(share, order[k])
        gate = add(gate, nn(h, wg[rows, :]))
        up = add(up, nn(h, wu[rows, :]))
    r2 = lax.rsqrt(jnp.sum(squares, axis=-1, keepdims=True) / (n * share) + EPS)
    g_hidden = nt(cot[...], wd[...])
    gate = gate * r2
    up = up * r2
    sig = jax.nn.sigmoid(gate)
    silu = gate * sig
    hidden[...] = (silu * up).astype(BF)
    g_gate = g_hidden * up * sig * (1.0 + gate * (1.0 - sig))
    g_up = g_hidden * silu
    m2[...] = row_sums(g_gate * gate + g_up * up)
    g_gate = (g_gate * r2).astype(BF)
    g_up = (g_up * r2).astype(BF)
    g_gu[:, :hid] = g_gate
    g_gu[:, hid:] = g_up
    r2_out[...] = jnp.broadcast_to(r2, r2_out.shape)
    for k in range(n):
        rows = tiles(share, order[k])
        pieces[k][...] = (nt(g_gate, wg[rows, :]) + nt(g_up, wu[rows, :])).astype(BF)


def call_ffn(order, c, hs, cot, inv_gain, wg, wu, wd):
    n = len(hs)
    rows, share = hs[0].shape
    hid = wg.shape[1]
    bt = min(rows, 256)
    steps = rows // bt

    def row(w, skip=0):
        return pl.BlockSpec((bt, w), lambda i, o: (i + skip, 0))

    def full(a):
        return pl.BlockSpec(a.shape, lambda i, o: (0, 0))

    spec = pltpu.PrefetchScalarGridSpec(
        num_scalar_prefetch=1,
        grid=(steps,),
        in_specs=[row(share)] * n
        + [row(n * share, c * steps)]
        + [full(a) for a in (inv_gain, wg, wu, wd)],
        out_specs=[row(hid), row(2 * hid), row(128), pl.BlockSpec((8, bt), lambda i, o: (0, i))]
        + [row(share)] * n,
    )
    return pl.pallas_call(
        functools.partial(ffn_kernel, n),
        grid_spec=spec,
        out_shape=[
            shape((rows, hid), BF),
            shape((rows, 2 * hid), BF),
            shape((rows, 128), F32),
            shape((8, rows), F32),
        ]
        + [shape((rows, share), BF)] * n,
        compiler_params=params(),
        cost_estimate=cost(2 * 5 * rows * n * share * hid, 14 * rows * n * share),
        name="ffn",
    )(order, *hs, cot, inv_gain, wg, wu, wd)


def down_kernel(n, order, hidden, wd, *pieces):
    share = wd.shape[1] // n
    for k in range(n):
        pieces[k][...] = nn(hidden[...], wd[:, tiles(share, order[k])]).astype(BF)


def call_down(order, hidden, wd):
    n = order.shape[0]
    rows, share = hidden.shape[0], wd.shape[1] // n
    return pl.pallas_call(
        functools.partial(down_kernel, n),
        out_shape=[shape((rows, share), BF)] * n,
        in_specs=[SM, VM, VM],
        out_specs=[VM] * n,
        compiler_params=params(),
        cost_estimate=cost(3 * rows * n * share * hidden.shape[1], 4 * rows * n * share),
        name="down",
    )(order, hidden, wd)


def g_mixed_kernel(n, order, wo, *refs):
    rights, g_mixed = refs[:-1], refs[-1]
    rows, share = rights[0].shape
    for c in range(len(rights) // n):
        total = None
        for k in range(n):
            total = add(total, nt(rights[c * n + k][...], wo[:, tiles(share, order[k])]))
        g_mixed[c * rows : (c + 1) * rows, :] = total.astype(BF)


def call_g_mixed(order, wo, rights):
    n = order.shape[0]
    tok = rights[0].shape[0] * len(rights) // n
    return pl.pallas_call(
        functools.partial(g_mixed_kernel, n),
        out_shape=shape((tok, wo.shape[0]), BF),
        in_specs=[SM, VM] + [VM] * len(rights),
        out_specs=VM,
        compiler_params=params(),
        cost_estimate=cost(5 * tok * wo.shape[0] * wo.shape[1], 4 * tok * wo.shape[1]),
        name="g_mixed",
    )(order, wo, *rights)


def gate_grad_kernel(n, chunks, order, *refs):
    lefts, gs, out_g, out_u = refs[: n * chunks], refs[n * chunks : -2], refs[-2], refs[-1]
    share, hid = lefts[0].shape[1], out_g.shape[1]
    for k in range(n):
        total = None
        for c in range(chunks):
            total = add(total, tn(lefts[c * n + k][...], gs[c][...]))
        rows = tiles(share, order[k])
        out_g[rows, :] = total[:, :hid].astype(BF)
        out_u[rows, :] = total[:, hid:].astype(BF)


def call_gate_grad(order, lefts, gs):
    n, chunks = order.shape[0], len(gs)
    dims = (n * lefts[0].shape[1], gs[0].shape[1] // 2)
    return pl.pallas_call(
        functools.partial(gate_grad_kernel, n, chunks),
        out_shape=[shape(dims, BF)] * 2,
        in_specs=[SM] + [VM] * (len(lefts) + chunks),
        out_specs=[VM, VM],
        compiler_params=params(),
        cost_estimate=cost(2 * chunks * gs[0].shape[0] * gs[0].shape[1] * dims[0], 4 * chunks * gs[0].shape[0] * dims[0]),
        name="grad_gate_up",
    )(order, *lefts, *gs)


def down_grad_kernel(n, per, order, cot, *refs):
    hiddens, out = refs[:-1], refs[-1]
    share, (rows, hid) = cot.shape[1] // n, hiddens[0].shape
    for k in range(n):
        total = None
        for c, hidden in enumerate(hiddens):
            total = add(total, tn(hidden[...], cot[c * rows : (c + 1) * rows, k * share : (k + 1) * share]))
        at, col = (k // per) * hid, (k % per) * share
        out[at : at + hid, col : col + share] = total.astype(BF)


def call_down_grad(order, per, cot, hiddens):
    n = order.shape[0]
    share, hid = cot.shape[1] // n, hiddens[0].shape[1]
    return pl.pallas_call(
        functools.partial(down_grad_kernel, n, per),
        out_shape=shape((n // per * hid, per * share), BF),
        in_specs=[SM, VM] + [VM] * len(hiddens),
        out_specs=VM,
        compiler_params=params(),
        cost_estimate=cost(3 * cot.shape[0] * cot.shape[1] * hid, 4 * cot.shape[0] * cot.shape[1]),
        name="grad_down",
    )(order, cot, *hiddens)


def qkv_back_kernel(n, n_far, order, g_query, g_kv, q, kv, cos, sin, wq, wk, wv, *refs):
    arrived, g_qkv, m1, pieces = refs[:n_far], refs[n_far], refs[n_far + 1], refs[n_far + 2 :]
    share = wq.shape[0] // n
    total = g_kv[...]
    for a in arrived:
        total = total + a[...].astype(F32)
    gq, gk, gv = g_query[...] * SCALE, total[:, :HDIM], total[:, HDIM:]
    m1[...] = row_sums(
        gq * q[...].astype(F32) + gk * kv[:, :HDIM].astype(F32) + gv * kv[:, HDIM:].astype(F32)
    )
    c, s = cos[...], sin[...]

    def back(v):
        return (v * c - pltpu.roll(v, HDIM // 2, 1) * s).astype(BF)

    gq, gk, gv = back(gq), back(gk), gv.astype(BF)
    g_qkv[:, :HDIM] = gq
    g_qkv[:, HDIM : 2 * HDIM] = gk
    g_qkv[:, 2 * HDIM :] = gv
    for k in range(n):
        rows = tiles(share, order[k])
        pieces[k][...] = (nt(gq, wq[rows, :]) + nt(gk, wk[rows, :]) + nt(gv, wv[rows, :])).astype(BF)


def call_qkv_back(order, g_query, g_kv, q, kv, cos, sin, wq, wk, wv, arrived):
    n, n_far = order.shape[0], len(arrived)
    tok = q.shape[0]
    bt = min(tok, 256)

    def row(w):
        return pl.BlockSpec((bt, w), lambda i, o: (i, 0))

    def full(a):
        return pl.BlockSpec(a.shape, lambda i, o: (0, 0))

    share = wq.shape[0] // n
    spec = pltpu.PrefetchScalarGridSpec(
        num_scalar_prefetch=1,
        grid=(tok // bt,),
        in_specs=[row(HDIM), row(2 * HDIM), row(HDIM), row(2 * HDIM), row(HDIM), row(HDIM)]
        + [full(a) for a in (wq, wk, wv)]
        + [row(2 * HDIM)] * n_far,
        out_specs=[row(3 * HDIM), pl.BlockSpec((8, bt), lambda i, o: (0, i))] + [row(share)] * n,
    )
    return pl.pallas_call(
        functools.partial(qkv_back_kernel, n, n_far),
        grid_spec=spec,
        out_shape=[shape((tok, 3 * HDIM), BF), shape((8, tok), F32)] + [shape((tok, share), BF)] * n,
        compiler_params=params(),
        cost_estimate=cost(6 * tok * n * share * 3 * HDIM, 4 * tok * n * share),
        name="qkv_back",
    )(order, g_query, g_kv, q, kv, cos, sin, wq, wk, wv, *arrived)


def tail_grad_kernel(n, chunks, order, left, g_qkv, *refs):
    mixed, rights, out = refs[:chunks], refs[chunks:-1], refs[-1]
    share, rows = left.shape[1] // n, mixed[0].shape[0]
    for k in range(n):
        at = tiles(share, order[k])
        out[at, : 3 * HDIM] = tn(left[:, k * share : (k + 1) * share], g_qkv[...]).astype(BF)
        total = None
        for c in range(chunks):
            total = add(total, tn(rights[c * n + k][...], mixed[c][...]))
        out[at, 3 * HDIM :] = total.astype(BF)


def call_tail_grad(order, left, g_qkv, mixed, rights):
    n, chunks = order.shape[0], len(mixed)
    return pl.pallas_call(
        functools.partial(tail_grad_kernel, n, chunks),
        out_shape=shape((left.shape[1], 4 * HDIM), BF),
        in_specs=[SM] + [VM] * (2 + chunks + len(rights)),
        out_specs=VM,
        compiler_params=params(),
        cost_estimate=cost(4 * left.shape[0] * left.shape[1] * 4 * HDIM, 4 * left.shape[0] * left.shape[1]),
        name="grad_tail",
    )(order, left, g_qkv, *mixed, *rights)


def folded(n):
    return [0] + list(range(1, n, 2)) + list(range(n - 2 + n % 2, 0, -2))


class Tp:
    def __init__(self, n_tp):
        self.n = n_tp
        self.pairs = n_tp // 2
        ring = folded(self.pairs)
        place = [ring.index(z) for z in range(self.pairs)]
        self.core_perm = [(i, i ^ 1) for i in range(n_tp)]
        self.ring_to = []
        order = []
        for i in range(n_tp):
            z, c = divmod(i, 2)
            self.ring_to.append(ring[(place[z] + 1) % self.pairs] * 2 + c)
            sources = [ring[(place[z] - j) % self.pairs] * 2 for j in range(self.pairs)]
            order.append([s + (c ^ b) for s in sources for b in (0, 1)])
        self.order = jnp.asarray(order, I32)[lax.axis_index("tp")]

    def core(self, a):
        return lax.ppermute(a, "tp", self.core_perm)

    def step(self, a, distance=1):
        perm = []
        for i in range(self.n):
            j = i
            for _ in range(distance):
                j = self.ring_to[j]
            perm.append((i, j))
        return lax.ppermute(a, "tp", perm)

    def gather(self, block, work=()):
        got, cur = [], block
        for j in range(self.pairs):
            if j == 2:
                cur = after(cur, *work)
            if j:
                cur = self.step(cur)
            got += [cur, self.core(cur)]
        return got

    def scatter(self, pieces, small=None, work=()):
        if small is not None:
            small = small + self.core(small)
            small = sum([self.step(small, d) for d in range(1, self.pairs)], small)
        acc, held, done = None, (), []
        for hop, j in enumerate(list(range(1, self.pairs)) + [0]):
            term = pieces[2 * j].astype(F32) + self.core(pieces[2 * j + 1]).astype(F32)
            if hop:
                acc = acc.astype(BF)
                if hop == 2 and small is not None:
                    acc, small = lax.optimization_barrier((acc, small))
                acc = after(acc, *held)
                held = ()
                if hop <= len(work):
                    held = work[hop - 1](acc)
                    done += held
                term = term + self.step(acc).astype(F32)
            acc = term
        if held:
            acc = after(acc, *held)
        return (acc, small, *done)


def after(value, *others):
    return lax.optimization_barrier((value, *others))[0]


def sum_ctx(a, n_ctx, rank):
    if n_ctx != 4:
        return lax.psum(a, "ctx")

    def halves(a, bit):
        half = a.shape[0] // 2
        keep = lax.dynamic_slice_in_dim(a, bit * half, half, 0)
        give = lax.dynamic_slice_in_dim(a, (1 - bit) * half, half, 0)
        return keep, give

    def swap(a, mask):
        return lax.ppermute(a, "ctx", [(r, r ^ mask) for r in range(4)])

    def joined(mine, got, bit):
        return jnp.where(bit == 0, jnp.concatenate([mine, got], 0), jnp.concatenate([got, mine], 0))

    bits = (rank % 2, rank // 2)
    rows = a.shape[0] // 2
    parts = []
    for part, first in ((a[:rows], 0), (a[rows:], 1)):
        for axis in (first, 1 - first):
            keep, give = halves(part, bits[axis])
            part = (keep.astype(F32) + swap(give, 1 << axis).astype(F32)).astype(BF)
        for axis in (1 - first, first):
            part = joined(part, swap(part, 1 << axis), bits[axis])
        parts.append(part)
    return jnp.concatenate(parts, axis=0)


def per_device(
    layer_in,
    gain_attn,
    gain_ffn,
    w_query,
    w_key,
    w_value,
    w_out,
    w_gate,
    w_up,
    w_down,
    doc_ids,
    positions,
    cotangent,
):
    tok, share = layer_in.shape
    n_ctx, n_tp = lax.axis_size("ctx"), lax.axis_size("tp")
    width = share * n_tp
    tp = Tp(n_tp)
    order = tp.order
    rank = lax.axis_index("ctx").astype(I32)
    own = lax.axis_index("tp") * share
    bias = -math.log(tok * n_ctx)
    rows = tok // CHUNKS
    parts = [slice(c * rows, (c + 1) * rows) for c in range(CHUNKS)]
    gain_a_own = lax.dynamic_slice_in_dim(gain_attn, own, share, 0)
    gain_f_own = lax.dynamic_slice_in_dim(gain_ffn, own, share, 0)

    def shift(a, s):
        return lax.ppermute(a, "ctx", [(r, r + s) for r in range(n_ctx) if 0 <= r + s < n_ctx])

    def broad(a):
        return jnp.tile(a, (1, share // a.shape[1]))

    per = max(1, min(4 * HDIM // share, n_tp))

    freq = THETA ** (-(jnp.arange(HDIM // 2, dtype=F32) * 2.0 / HDIM))
    angle = positions.astype(F32)[:, None] * freq[None, :]
    cos, sin = jnp.cos(angle), jnp.sin(angle)
    cos, sin = jnp.concatenate([cos, cos], 1), jnp.concatenate([-sin, sin], 1)
    q_start = rank * tok + jnp.arange(tok, dtype=I32) - positions
    edges = edges_of(rank, tok, q_start)
    gain_blocks, inv_gain = gain_attn.reshape(n_tp, share), (1.0 / gain_ffn).reshape(n_tp, share)
    start_col, start_row = q_start[:, None], q_start[None, :]
    prepared = lax.optimization_barrier((cos, sin, edges, start_col, start_row, gain_blocks, inv_gain, order))
    cos, sin, edges, start_col, start_row, gain_blocks, inv_gain, order = prepared
    xs = tp.gather(layer_in, prepared)
    normed, q_rot, kv_own, r1 = call_qkv(order, xs, gain_blocks, w_query, w_key, w_value, cos, sin)
    cot_full = lax.all_gather(after(cotangent, xs[-2]), "tp", axis=1, tiled=True)
    kv_far = [shift(kv_own, s) for s in range(1, n_ctx)]
    acc = call_own(bias, edges, start_col, q_rot, kv_own)
    mixed, hs, h_own = [], [], []
    for c, part in enumerate(parts):
        out, *pieces = call_far(bias, tok, c, rows, edges, order, start_col, q_rot, acc, w_out, kv_far)
        mixed.append(out)
        h = layer_in[part].astype(F32) + tp.scatter(pieces)[0]
        h_own.append(h)
        hs.append(tp.gather((h * gain_f_own).astype(BF)))

    hiddens, g_gus, g_hs, g_hbs = [], [], [], []
    grad_gain_two = 0.0
    for c, part in enumerate(parts):
        hidden, g_gu, r2, m2, *pieces = call_ffn(order, c, hs[c], cot_full, inv_gain, w_gate, w_up, w_down)
        hiddens.append(hidden)
        g_gus.append(g_gu)
        work = ()
        if c == CHUNKS - 1:

            def grads_1(sent):
                return call_gate_grad(order, sum(hs, []), [after(g, sent) for g in g_gus])

            def grads_2(sent):
                return [call_down_grad(order, per, after(cot_full, sent), hiddens)]

            work = (grads_1, grads_2)
        dn2, m2, *grads = tp.scatter(pieces, m2[0], work)
        m2 = m2 / width
        r2 = broad(r2)
        g_h = cotangent[part].astype(F32) + gain_f_own * dn2 - (r2 * r2 * m2[:, None]) * h_own[c]
        grad_gain_two = grad_gain_two + jnp.sum(dn2 * h_own[c], axis=0)
        g_hs.append(g_h)
        g_hbs.append(tp.gather(g_h.astype(BF)))

    hidden = jnp.concatenate(hiddens, 0)
    grad_gate, grad_up, grad_down = lax.psum(tuple(grads), "ctx")
    down = call_down(order, hidden, w_down)
    g_hbs[-1][-2], *down = lax.optimization_barrier((g_hbs[-1][-2], *down))
    g_mixed = call_g_mixed(order, w_out, sum(g_hbs, []))
    g_query, *g_kv_far = call_far_back(bias, edges, start_row, q_rot, g_mixed, kv_far)
    arrived = [shift(g, -s) for s, g in zip(range(1, n_ctx), g_kv_far)]
    g_query, g_kv = call_own_back(bias, edges, start_row, q_rot, g_mixed, kv_own, g_query)
    down = tp.scatter(down)[0]
    outs = (jnp.concatenate(h_own, 0) + down).astype(BF)
    g_kv = after(g_kv, outs, grad_gate, grad_up, grad_down)
    g_qkv, m1, *pieces = call_qkv_back(
        order, g_query, g_kv, q_rot, kv_own, cos, sin, w_query, w_key, w_value, arrived
    )

    def grads_3(sent):
        return [call_tail_grad(order, normed, after(g_qkv, sent), mixed, sum(g_hbs, []))]

    dn1, m1, tail = tp.scatter(pieces, m1[0], (grads_3,))
    m1 = m1 / width
    r1 = broad(r1)
    x_hat = layer_in.astype(F32) * r1
    g_input = jnp.concatenate(g_hs, 0) + r1 * (dn1 * gain_a_own - x_hat * m1[:, None])
    grad_gain_one = jnp.sum(dn1 * x_hat, axis=0)

    tail = sum_ctx(tail, n_ctx, rank).astype(F32)
    hid = w_gate.shape[1]
    down_blocks = [grad_down[i * hid : (i + 1) * hid] for i in range(n_tp // per)]
    gains = jnp.concatenate([grad_gain_one, grad_gain_two])
    gains = sum(
        [lax.ppermute(gains, "ctx", [(r, (r + s) % n_ctx) for r in range(n_ctx)]) for s in range(1, n_ctx)],
        gains,
    )
    return (
        outs,
        g_input,
        gains[:share],
        gains[share:],
        tail[:, :HDIM],
        tail[:, HDIM : 2 * HDIM],
        tail[:, 2 * HDIM : 3 * HDIM],
        tail[:, 3 * HDIM :].T,
        grad_gate.astype(F32),
        grad_up.astype(F32),
        jnp.concatenate(down_blocks, 1).astype(F32),
    )


def solution(mesh):
    row, col = P("tp", None), P(None, "tp")
    both = P("ctx", "tp")
    in_specs = (both, P(), P(), col, col, col, row, col, col, row, P("ctx"), P("ctx"), both)
    out_specs = (both, both, P("tp"), P("tp"), col, col, col, row, col, col, row)
    return jax.shard_map(
        per_device, mesh=mesh, in_specs=in_specs, out_specs=out_specs, check_vma=False
    )
```

```python
import functools
import math

import jax
import jax.numpy as jnp
from jax import lax
from jax.experimental import pallas as pl
from jax.experimental.pallas import tpu as pltpu
from jax.sharding import PartitionSpec as P

HDIM = 128
EPS = 1e-05
THETA = 10000.0
LOG2E = math.log2(math.e)
SCALE = 1.0 / math.sqrt(HDIM)
BF = jnp.bfloat16
F32 = jnp.float32
I32 = jnp.int32
BQ, BK = 512, 512
VMEM_BYTES = 60 * 1024 * 1024
COST = 1.0

SM = pl.BlockSpec(memory_space=pltpu.SMEM)
VM = pl.BlockSpec(memory_space=pltpu.VMEM)


def shape(dims, dtype):
    return jax.ShapeDtypeStruct(dims, dtype)


def params():
    return pltpu.CompilerParams(vmem_limit_bytes=VMEM_BYTES)


def cost(mults, size):
    return pl.CostEstimate(flops=int(2 * mults * COST), bytes_accessed=int(size * COST), transcendentals=0)


def nn(a, b):
    return lax.dot_general(a, b, (((1,), (0,)), ((), ())), preferred_element_type=F32)


def nt(a, b):
    return lax.dot_general(a, b, (((1,), (1,)), ((), ())), preferred_element_type=F32)


def tn(a, b):
    return lax.dot_general(a, b, (((0,), (0,)), ((), ())), preferred_element_type=F32)


def add(a, b):
    return b if a is None else a + b


def tiles(width, k, n=None):
    return pl.ds(pl.multiple_of(k * width, width), width)


def row_sums(a):
    high = a.astype(BF)
    low = (a - high.astype(F32)).astype(BF)
    ones = jnp.ones((8, a.shape[1]), BF)
    return nt(ones, high) + nt(ones, low)


def qkv_kernel(n, order, *refs):
    xs = refs[:n]
    gain, wq, wk, wv, cos, sin, normed, q, kv, r1_out = refs[n:]
    share = xs[0].shape[1]
    squares = None
    for k in range(n):
        v = xs[k][...].astype(F32)
        squares = add(squares, v * v)
    r1 = lax.rsqrt(jnp.sum(squares, axis=-1, keepdims=True) / (n * share) + EPS)
    sums = [None] * 3
    for k in range(n):
        block = (xs[k][...].astype(F32) * r1 * gain[pl.ds(order[k], 1), :]).astype(BF)
        normed[:, k * share : (k + 1) * share] = block
        rows = tiles(share, order[k])
        for i, w in enumerate((wq, wk, wv)):
            sums[i] = add(sums[i], nn(block, w[rows, :]))
    c, s = cos[...], sin[...]

    def rotated(v):
        return v * c + pltpu.roll(v, HDIM // 2, 1) * s

    q[...] = rotated(sums[0]).astype(BF)
    kv[:, :HDIM] = rotated(sums[1]).astype(BF)
    kv[:, HDIM:] = sums[2].astype(BF)
    r1_out[...] = jnp.broadcast_to(r1, r1_out.shape)


def call_qkv(order, xs, gain, wq, wk, wv, cos, sin):
    n = len(xs)
    tok, share = xs[0].shape
    bt = min(tok, 256)

    def row(w):
        return pl.BlockSpec((bt, w), lambda i, o: (i, 0))

    def full(a):
        return pl.BlockSpec(a.shape, lambda i, o: (0, 0))

    spec = pltpu.PrefetchScalarGridSpec(
        num_scalar_prefetch=1,
        grid=(tok // bt,),
        in_specs=[row(share)] * n + [full(a) for a in (gain, wq, wk, wv)] + [row(HDIM)] * 2,
        out_specs=[row(n * share), row(HDIM), row(2 * HDIM), row(128)],
    )
    return pl.pallas_call(
        functools.partial(qkv_kernel, n),
        grid_spec=spec,
        out_shape=[
            shape((tok, n * share), BF),
            shape((tok, HDIM), BF),
            shape((tok, 2 * HDIM), BF),
            shape((tok, 128), F32),
        ],
        compiler_params=params(),
        cost_estimate=cost(5 * tok * n * share * HDIM * 4, 10 * tok * n * share),
        name="norm_qkv",
    )(order, *xs, gain, wq, wk, wv, cos, sin)


def edges_of(rank, tok, starts):
    t = starts.reshape(tok // BQ, BQ)
    return jnp.concatenate([(rank * tok)[None], jnp.stack([t[:, 0], t[:, -1]], axis=1).reshape(-1)])


def sigmoid_of(raw, bias):
    return 1.0 / (1.0 + jnp.exp2(raw * (-LOG2E * SCALE) - bias * LOG2E))


def own_kernel(bias, tok, edges, start, q, kv, total):
    base = edges[0]
    for qi in range(tok // BQ):
        rows = slice(qi * BQ, (qi + 1) * BQ)
        q_tile = q[rows, :]
        first_key = start[rows, :] - base
        q_index = qi * BQ + lax.broadcasted_iota(I32, (BQ, 1), 0)

        def body(ki, acc):
            at = tiles(BK, ki)
            w = sigmoid_of(nt(q_tile, kv[at, :HDIM]), bias)
            k_index = ki * BK + lax.broadcasted_iota(I32, (BQ, BK), 1)
            w = jnp.where((k_index >= first_key) & (k_index <= q_index), w, 0.0)
            return acc + nn(w.astype(BF), kv[at, HDIM:])

        low = jnp.maximum(edges[1 + 2 * qi] - base, 0) // BK
        high = ((qi + 1) * BQ + BK - 1) // BK
        total[rows, :] = lax.fori_loop(low, high, body, jnp.zeros((BQ, HDIM), F32))


def far_kernel(bias, tok, q0, n_far, n, edges, order, start, q, acc, wo, *refs):
    kvs, mixed, pieces = refs[:n_far], refs[n_far], refs[n_far + 1 :]
    share = wo.shape[1] // n
    n_keys = tok // BK
    for qi in range(q.shape[0] // BQ):
        rows = slice(qi * BQ, (qi + 1) * BQ)
        at_first, at_last = 1 + 2 * (q0 // BQ + qi), 2 + 2 * (q0 // BQ + qi)
        q_tile = q[rows, :]
        total = acc[rows, :]
        for i in range(n_far):
            base = edges[0] - (i + 1) * tok
            kv = kvs[i]
            first_key = start[rows, :] - base

            def body(ki, total, masked):
                at = tiles(BK, ki)
                w = sigmoid_of(nt(q_tile, kv[at, :HDIM]), bias)
                if masked:
                    k_index = ki * BK + lax.broadcasted_iota(I32, (BQ, BK), 1)
                    w = jnp.where(k_index >= first_key, w, 0.0)
                return total + nn(w.astype(BF), kv[at, HDIM:])

            low = jnp.clip(edges[at_first] - base, 0, tok) // BK
            mid = jnp.clip(edges[at_last] - base + BK - 1, 0, tok) // BK
            mid = jnp.maximum(low, mid)
            total = lax.fori_loop(low, mid, functools.partial(body, masked=True), total)
            total = lax.fori_loop(mid, n_keys, functools.partial(body, masked=False), total)
        rounded = total.astype(BF)
        mixed[rows, :] = rounded
        for k in range(n):
            pieces[k][rows, :] = nn(rounded, wo[:, tiles(share, order[k])]).astype(BF)


def tile_back(bias, q_tile, g_tile, k_tile, v_tile, keep, g_query, rows, sums):
    s = sigmoid_of(nt(k_tile, q_tile), bias)
    g_weight = nt(v_tile, g_tile)
    if keep is not None:
        s = jnp.where(keep, s, 0.0)
    g_s = (g_weight * (s * (1.0 - s))).astype(BF)
    g_value = sums[1] + nn(s.astype(BF), g_tile)
    g_key = sums[0] + nn(g_s, q_tile)
    g_query[rows, :] = g_query[rows, :] + tn(g_s, k_tile)
    return g_key, g_value


def count_tiles(edges, n_q, which, limit):
    return sum([(edges[which + 2 * i] <= limit).astype(I32) for i in range(n_q)], jnp.int32(0))


def far_back_kernel(bias, tok, n_far, edges, start, q, g, *refs):
    kvs, g_query, outs = refs[:n_far], refs[n_far], refs[n_far + 1 :]
    n_q = tok // BQ
    g_query[...] = jnp.zeros_like(g_query)
    for i in reversed(range(n_far)):
        base = edges[0] - (i + 1) * tok
        kv, out = kvs[i], outs[i]

        def key_tile(ki, carry):
            at = tiles(BK, ki)
            k_tile, v_tile = kv[at, :HDIM], kv[at, HDIM:]
            key0 = base + ki * BK
            high = count_tiles(edges, n_q, 1, key0 + BK - 1)
            mid = count_tiles(edges, n_q, 2, key0)

            def body(qi, sums, masked):
                r = tiles(BQ, qi)
                keep = None
                if masked:
                    keep = key0 + lax.broadcasted_iota(I32, (BK, BQ), 0) >= start[:, r]
                return tile_back(bias, q[r, :], g[r, :], k_tile, v_tile, keep, g_query, r, sums)

            zero = jnp.zeros((BK, HDIM), F32)
            sums = lax.fori_loop(0, mid, functools.partial(body, masked=False), (zero, zero))
            g_key, g_value = lax.fori_loop(mid, high, functools.partial(body, masked=True), sums)
            out[at, :HDIM] = (g_key * SCALE).astype(BF)
            out[at, HDIM:] = g_value.astype(BF)
            return carry

        live = jnp.logical_and(base >= 0, edges[1] <= base + tok - 1)

        @pl.when(live)
        def _():
            lax.fori_loop(0, tok // BK, key_tile, 0)

        @pl.when(jnp.logical_not(live))
        def _():
            out[...] = jnp.zeros_like(out)


def own_back_kernel(bias, tok, edges, start, q, g, kv, g_query_in, g_query, out):
    n_q = tok // BQ
    base = edges[0]
    g_query[...] = g_query_in[...]
    for ki in range(tok // BK):
        at = slice(ki * BK, (ki + 1) * BK)
        k_tile, v_tile = kv[at, :HDIM], kv[at, HDIM:]
        key0 = base + ki * BK

        def body(qi, sums):
            r = tiles(BQ, qi)
            k_index = key0 + lax.broadcasted_iota(I32, (BK, BQ), 0)
            q_index = base + qi * BQ + lax.broadcasted_iota(I32, (1, BQ), 1)
            keep = (k_index >= start[:, r]) & (k_index <= q_index)
            return tile_back(bias, q[r, :], g[r, :], k_tile, v_tile, keep, g_query, r, sums)

        zero = jnp.zeros((BK, HDIM), F32)
        high = count_tiles(edges, n_q, 1, key0 + BK - 1)
        g_key, g_value = lax.fori_loop((ki * BK) // BQ, high, body, (zero, zero))
        out[at, :HDIM] = g_key * SCALE
        out[at, HDIM:] = g_value


def call_own(bias, edges, start, q, kv):
    tok = q.shape[0]
    return pl.pallas_call(
        functools.partial(own_kernel, bias, tok),
        out_shape=shape((tok, HDIM), F32),
        in_specs=[SM, VM, VM, VM],
        out_specs=VM,
        compiler_params=params(),
        cost_estimate=cost(16 * tok * tok * HDIM, 4 * tok * HDIM),
        name="attend_own",
    )(edges, start, q, kv)


def call_far(bias, tok, c, rows, edges, order, start, q, acc, wo, kvs):
    n = order.shape[0]

    def part(w):
        return pl.BlockSpec((rows, w), lambda i: (c, 0))

    def full(a):
        return pl.BlockSpec(a.shape, lambda i: (0, 0))

    out = pl.BlockSpec((rows, HDIM), lambda i: (0, 0))
    share = wo.shape[1] // n
    return pl.pallas_call(
        functools.partial(far_kernel, bias, tok, c * rows, len(kvs), n),
        grid=(1,),
        out_shape=[shape((rows, HDIM), BF)] + [shape((rows, share), BF)] * n,
        in_specs=[SM, SM, part(1), part(HDIM), part(HDIM), full(wo)] + [full(a) for a in kvs],
        out_specs=[out] + [pl.BlockSpec((rows, share), lambda i: (0, 0))] * n,
        compiler_params=params(),
        cost_estimate=cost(20 * rows * tok * HDIM + 12 * rows * n * share * HDIM, 4 * rows * n * share),
        name="attend_far",
    )(edges, order, start, q, acc, wo, *kvs)


def call_far_back(bias, edges, start, q, g, kvs):
    tok = q.shape[0]
    return pl.pallas_call(
        functools.partial(far_back_kernel, bias, tok, len(kvs)),
        out_shape=[shape((tok, HDIM), F32)] + [shape((tok, 2 * HDIM), BF)] * len(kvs),
        in_specs=[SM] + [VM] * (3 + len(kvs)),
        out_specs=[VM] * (1 + len(kvs)),
        compiler_params=params(),
        cost_estimate=cost(48 * tok * tok * HDIM, 16 * tok * HDIM),
        name="attend_far_back",
    )(edges, start, q, g, *kvs)


def call_own_back(bias, edges, start, q, g, kv, g_query):
    tok = q.shape[0]
    return pl.pallas_call(
        functools.partial(own_back_kernel, bias, tok),
        out_shape=[shape((tok, HDIM), F32), shape((tok, 2 * HDIM), F32)],
        in_specs=[SM] + [VM] * 5,
        out_specs=[VM] * 2,
        compiler_params=params(),
        cost_estimate=cost(28 * tok * tok * HDIM, 16 * tok * HDIM),
        name="attend_own_back",
    )(edges, start, q, g, kv, g_query)


def ffn_kernel(n, order, *refs):
    hs = refs[:n]
    cot, inv_gain, wg, wu, wd, hidden, g_gu, r2_out, m2, back = refs[n:]
    share, hid = hs[0].shape[1], wg.shape[1]
    squares = gate = up = None
    for k in range(n):
        h = hs[k][...]
        v = h.astype(F32) * inv_gain[pl.ds(order[k], 1), :]
        squares = add(squares, v * v)
        rows = tiles(share, order[k])
        gate = add(gate, nn(h, wg[rows, :]))
        up = add(up, nn(h, wu[rows, :]))
    r2 = lax.rsqrt(jnp.sum(squares, axis=-1, keepdims=True) / (n * share) + EPS)
    g_hidden = nt(cot[...], wd[...])
    gate = gate * r2
    up = up * r2
    sig = jax.nn.sigmoid(gate)
    silu = gate * sig
    hidden[...] = (silu * up).astype(BF)
    g_gate = g_hidden * up * sig * (1.0 + gate * (1.0 - sig))
    g_up = g_hidden * silu
    m2[...] = row_sums(g_gate * gate + g_up * up)
    g_gate = (g_gate * r2).astype(BF)
    g_up = (g_up * r2).astype(BF)
    g_gu[:, :hid] = g_gate
    g_gu[:, hid:] = g_up
    r2_out[...] = jnp.broadcast_to(r2, r2_out.shape)
    for k in range(n):
        rows = slice(k * share, (k + 1) * share)
        back[:, rows] = (nt(g_gate, wg[rows, :]) + nt(g_up, wu[rows, :])).astype(BF)


def call_ffn(order, c, hs, cot, inv_gain, wg, wu, wd):
    n = len(hs)
    rows, share = hs[0].shape
    hid = wg.shape[1]
    bt = min(rows, 256)
    steps = rows // bt

    def row(w, skip=0):
        return pl.BlockSpec((bt, w), lambda i, o: (i + skip, 0))

    def full(a):
        return pl.BlockSpec(a.shape, lambda i, o: (0, 0))

    spec = pltpu.PrefetchScalarGridSpec(
        num_scalar_prefetch=1,
        grid=(steps,),
        in_specs=[row(share)] * n
        + [row(n * share, c * steps)]
        + [full(a) for a in (inv_gain, wg, wu, wd)],
        out_specs=[row(hid), row(2 * hid), row(128), pl.BlockSpec((8, bt), lambda i, o: (0, i)), row(n * share)],
    )
    return pl.pallas_call(
        functools.partial(ffn_kernel, n),
        grid_spec=spec,
        out_shape=[
            shape((rows, hid), BF),
            shape((rows, 2 * hid), BF),
            shape((rows, 128), F32),
            shape((8, rows), F32),
            shape((rows, n * share), BF),
        ],
        compiler_params=params(),
        cost_estimate=cost(2 * 5 * rows * n * share * hid, 14 * rows * n * share),
        name="ffn",
    )(order, *hs, cot, inv_gain, wg, wu, wd)


def put(parts, bits, row, rows, cols, value):
    size = parts.shape[1]
    quarter = row // size
    half = quarter // 2
    goes = (quarter % 2 != bits[half]).astype(I32)
    at = pl.ds(pl.multiple_of(row - quarter * size, rows), rows)
    parts[half * 2 + goes, at, cols] = value


def ffn_grad_kernel(n, per, order, bits, cot, *refs):
    lefts, g_gu, hidden, outs, parts = refs[:n], refs[n], refs[n + 1], refs[n + 2 : -1], refs[-1]
    share, wide, hid = lefts[0].shape[1], g_gu.shape[1], hidden.shape[1]
    step = min(hid, parts.shape[1])
    for k in range(n):
        value = tn(lefts[k][...], g_gu[...]).astype(BF)
        put(parts, bits, order[k] * share, share, slice(0, wide), value)
        row, col = (k // per) * hid, wide + (k % per) * share
        value = tn(hidden[...], cot[:, k * share : (k + 1) * share]).astype(BF)
        for r in range(0, hid, step):
            put(parts, bits, jnp.int32(row + r), step, slice(col, col + share), value[r : r + step, :])
    for i, out in enumerate(outs):
        out[...] = parts[i]


def call_ffn_grad(order, bits, per, cot, lefts, g_gu, hidden):
    n = order.shape[0]
    wide = g_gu.shape[1] + per * lefts[0].shape[1]
    return pl.pallas_call(
        functools.partial(ffn_grad_kernel, n, per),
        out_shape=[shape((cot.shape[1] // 4, wide), BF)] * 4,
        in_specs=[SM, SM] + [VM] * (3 + len(lefts)),
        out_specs=[VM] * 4,
        scratch_shapes=[pltpu.VMEM((4, cot.shape[1] // 4, wide), BF)],
        compiler_params=params(),
        cost_estimate=cost(2 * cot.shape[0] * cot.shape[1] * wide, 8 * cot.shape[0] * cot.shape[1]),
        name="grad_ffn",
    )(order, bits, cot, *lefts, g_gu, hidden)


def qkv_back_kernel(n, n_far, g_query, g_kv, q, kv, cos, sin, wq, wk, wv, *refs):
    arrived, (g_qkv, m1, out) = refs[:n_far], refs[n_far:]
    share = wq.shape[0] // n
    total = g_kv[...]
    for a in arrived:
        total = total + a[...].astype(F32)
    gq, gk, gv = g_query[...] * SCALE, total[:, :HDIM], total[:, HDIM:]
    m1[...] = row_sums(
        gq * q[...].astype(F32) + gk * kv[:, :HDIM].astype(F32) + gv * kv[:, HDIM:].astype(F32)
    )
    c, s = cos[...], sin[...]

    def back(v):
        return (v * c - pltpu.roll(v, HDIM // 2, 1) * s).astype(BF)

    gq, gk, gv = back(gq), back(gk), gv.astype(BF)
    g_qkv[:, :HDIM] = gq
    g_qkv[:, HDIM : 2 * HDIM] = gk
    g_qkv[:, 2 * HDIM :] = gv
    for k in range(n):
        rows = slice(k * share, (k + 1) * share)
        out[:, rows] = (nt(gq, wq[rows, :]) + nt(gk, wk[rows, :]) + nt(gv, wv[rows, :])).astype(BF)


def call_qkv_back(n, g_query, g_kv, q, kv, cos, sin, wq, wk, wv, arrived):
    n_far = len(arrived)
    tok = q.shape[0]
    bt = min(tok, 256)

    def row(w):
        return pl.BlockSpec((bt, w), lambda i: (i, 0))

    def full(a):
        return pl.BlockSpec(a.shape, lambda i: (0, 0))

    width = wq.shape[0]
    return pl.pallas_call(
        functools.partial(qkv_back_kernel, n, n_far),
        grid=(tok // bt,),
        in_specs=[row(HDIM), row(2 * HDIM), row(HDIM), row(2 * HDIM), row(HDIM), row(HDIM)]
        + [full(a) for a in (wq, wk, wv)]
        + [row(2 * HDIM)] * n_far,
        out_specs=[row(3 * HDIM), pl.BlockSpec((8, bt), lambda i: (0, i)), row(width)],
        out_shape=[shape((tok, 3 * HDIM), BF), shape((8, tok), F32), shape((tok, width), BF)],
        compiler_params=params(),
        cost_estimate=cost(6 * tok * width * 3 * HDIM, 4 * tok * width),
        name="qkv_back",
    )(g_query, g_kv, q, kv, cos, sin, wq, wk, wv, *arrived)


def tail_grad_kernel(n, order, bits, left, g_qkv, mixed, g_hb, *refs):
    outs, parts = refs[:-1], refs[-1]
    share = left.shape[1] // n
    for k in range(n):
        block = slice(k * share, (k + 1) * share)
        value = tn(left[:, block], g_qkv[...]).astype(BF)
        put(parts, bits, order[k] * share, share, slice(0, 3 * HDIM), value)
        value = tn(g_hb[:, block], mixed[...]).astype(BF)
        put(parts, bits, jnp.int32(k * share), share, slice(3 * HDIM, 4 * HDIM), value)
    for i, out in enumerate(outs):
        out[...] = parts[i]


def call_tail_grad(order, bits, left, g_qkv, mixed, g_hb):
    return pl.pallas_call(
        functools.partial(tail_grad_kernel, order.shape[0]),
        out_shape=[shape((left.shape[1] // 4, 4 * HDIM), BF)] * 4,
        in_specs=[SM, SM] + [VM] * 4,
        out_specs=[VM] * 4,
        scratch_shapes=[pltpu.VMEM((4, left.shape[1] // 4, 4 * HDIM), BF)],
        compiler_params=params(),
        cost_estimate=cost(4 * left.shape[0] * left.shape[1] * 4 * HDIM, 4 * left.shape[0] * left.shape[1]),
        name="grad_tail",
    )(order, bits, left, g_qkv, mixed, g_hb)


def folded(n):
    return [0] + list(range(1, n, 2)) + list(range(n - 2 + n % 2, 0, -2))


class Tp:
    def __init__(self, n_tp):
        self.n = n_tp
        self.pairs = n_tp // 2
        ring = folded(self.pairs)
        place = [ring.index(z) for z in range(self.pairs)]
        self.core_perm = [(i, i ^ 1) for i in range(n_tp)]
        self.ring_to = []
        order = []
        for i in range(n_tp):
            z, c = divmod(i, 2)
            self.ring_to.append(ring[(place[z] + 1) % self.pairs] * 2 + c)
            sources = [ring[(place[z] - j) % self.pairs] * 2 for j in range(self.pairs)]
            order.append([s + (c ^ b) for s in sources for b in (0, 1)])
        self.order = jnp.asarray(order, I32)[lax.axis_index("tp")]

    def core(self, a):
        return lax.ppermute(a, "tp", self.core_perm)

    def step(self, a, distance=1):
        perm = []
        for i in range(self.n):
            j = i
            for _ in range(distance):
                j = self.ring_to[j]
            perm.append((i, j))
        return lax.ppermute(a, "tp", perm)

    def gather(self, block, gates=None):
        got, cur = [], block
        for j in range(self.pairs):
            if gates and j in gates:
                cur = after(cur, *gates[j](cur))
            if j:
                cur = self.step(cur)
            got += [cur, self.core(cur)]
        return got

    def scatter(self, pieces):
        acc = None
        for j in list(range(1, self.pairs)) + [0]:
            term = pieces[2 * j].astype(F32) + self.core(pieces[2 * j + 1]).astype(F32)
            if acc is not None:
                term = term + self.step(acc.astype(BF)).astype(F32)
            acc = term
        return acc

    def total(self, small):
        small = small + self.core(small)
        return sum([self.step(small, d) for d in range(1, self.pairs)], small)


def scatter_tp(a):
    return lax.psum_scatter(a, "tp", scatter_dimension=1, tiled=True)


def gather_tp(a):
    return lax.all_gather(a, "tp", axis=1, tiled=True)


def after(value, *others):
    return lax.optimization_barrier((value, *others))[0]


class SumCtx:
    def __init__(self, quarters, n_ctx, rank):
        self.n, self.bits = n_ctx, (rank % 2, rank // 2)
        self.quarters = quarters
        self.parts = [None, None] if n_ctx == 4 else [jnp.concatenate(quarters, 0)]
        self.phase = 0
        self.arrived = []

    def send(self):
        if self.n == 4:
            self.arrived = [self.swap(self.quarters[2 * i + 1], i) for i in (0, 1)]
        return self.arrived

    def swap(self, a, axis):
        return lax.ppermute(a, "ctx", [(r, r ^ (1 << axis)) for r in range(4)])

    def run(self, before=(), meanwhile=()):
        phase = self.phase
        self.phase += 1
        parts = [after(p, *before) for p in self.parts] if before else self.parts
        if self.n != 4:
            if phase == 0:
                self.parts = list(lax.psum(tuple(parts), "ctx"))
            return self.parts
        self.parts = []
        self.last = []
        for i, part in enumerate(parts):
            axis = (i + phase) % 2 if phase < 2 else (i + 1 + phase) % 2
            bit = self.bits[axis]
            give = part
            if phase == 0:
                part, give = self.quarters[2 * i : 2 * i + 2]
            elif phase == 1:
                half = part.shape[0] // 2
                give = lax.dynamic_slice_in_dim(part, (1 - bit) * half, half, 0)
                part = lax.dynamic_slice_in_dim(part, bit * half, half, 0)
            got = self.arrived[i] if phase == 0 and self.arrived else self.swap(give, axis)
            if meanwhile:
                got = after(got, *meanwhile)
            self.last.append((bit, part, got))
            if phase < 2:
                self.parts.append((part.astype(F32) + got.astype(F32)).astype(BF))
            elif phase == 2:
                self.parts.append(self.joined(bit, part, got))
        return self.parts or [got for _, _, got in self.last]

    def joined(self, bit, part, got):
        return jnp.where(bit == 0, jnp.concatenate([part, got], 0), jnp.concatenate([got, part], 0))

    def result(self, at, first=None, width=None):
        take = slice(None) if first is None else slice(first, first + width)
        if self.n != 4:
            return self.parts[at][:, take].astype(F32)
        both = [self.joined(bit, part[:, take], got[:, take]) for bit, part, got in self.last[2 * at : 2 * at + 2]]
        return jnp.concatenate(both, 0).astype(F32)


def per_device(
    layer_in,
    gain_attn,
    gain_ffn,
    w_query,
    w_key,
    w_value,
    w_out,
    w_gate,
    w_up,
    w_down,
    doc_ids,
    positions,
    cotangent,
):
    tok, share = layer_in.shape
    n_ctx, n_tp = lax.axis_size("ctx"), lax.axis_size("tp")
    width = share * n_tp
    tp = Tp(n_tp)
    order = tp.order
    rank = lax.axis_index("ctx").astype(I32)
    own = lax.axis_index("tp") * share
    bias = -math.log(tok * n_ctx)
    per = max(1, min(4 * HDIM // share, n_tp))
    bits = jnp.stack([rank % 2, rank // 2]) if n_ctx == 4 else jnp.zeros((2,), I32)
    gain_a_own = lax.dynamic_slice_in_dim(gain_attn, own, share, 0)
    gain_f_own = lax.dynamic_slice_in_dim(gain_ffn, own, share, 0)

    def shift(a, s):
        return lax.ppermute(a, "ctx", [(r, r + s) for r in range(n_ctx) if 0 <= r + s < n_ctx])

    def broad(a):
        return jnp.tile(a, (1, share // a.shape[1]))

    freq = THETA ** (-(jnp.arange(HDIM // 2, dtype=F32) * 2.0 / HDIM))
    angle = positions.astype(F32)[:, None] * freq[None, :]
    cos, sin = jnp.cos(angle), jnp.sin(angle)
    cos, sin = jnp.concatenate([cos, cos], 1), jnp.concatenate([-sin, sin], 1)
    q_start = rank * tok + jnp.arange(tok, dtype=I32) - positions
    edges = edges_of(rank, tok, q_start)
    gain_blocks, inv_gain = gain_attn.reshape(n_tp, share), (1.0 / gain_ffn).reshape(n_tp, share)
    start_col, start_row = q_start[:, None], q_start[None, :]
    prepared = lax.optimization_barrier((cos, sin, edges, start_col, start_row, gain_blocks, inv_gain, order))
    cos, sin, edges, start_col, start_row, gain_blocks, inv_gain, order = prepared
    xs = tp.gather(layer_in, {2: lambda arrived: prepared})
    normed, q_rot, kv_own, r1 = call_qkv(order, xs, gain_blocks, w_query, w_key, w_value, cos, sin)
    cot_full = lax.all_gather(after(cotangent, xs[-2]), "tp", axis=1, tiled=True)
    kv_far = [shift(kv_own, s) for s in range(1, n_ctx)]
    acc = call_own(bias, edges, start_col, q_rot, kv_own)
    mixed, *pieces = call_far(bias, tok, 0, tok, edges, order, start_col, q_rot, acc, w_out, kv_far)
    h = layer_in.astype(F32) + tp.scatter(pieces)
    hs = tp.gather((h * gain_f_own).astype(BF))

    hidden, g_gu, r2, m2, back = call_ffn(order, 0, hs, cot_full, inv_gain, w_gate, w_up, w_down)
    dn2 = scatter_tp(back)
    m2 = tp.total(m2[0]) / width
    grad_ffn = call_ffn_grad(order, bits, per, cot_full, hs, g_gu, hidden)
    ffn_sum = SumCtx(grad_ffn, n_ctx, rank)
    down = nn(hidden, after(w_down, grad_ffn[1])).astype(BF)
    dn2 = after(dn2, down, *ffn_sum.send()).astype(F32)
    r2 = broad(r2)
    g_h = cotangent.astype(F32) + gain_f_own * dn2 - (r2 * r2 * m2[:, None]) * h
    grad_gain_two = jnp.sum(dn2 * h, axis=0)
    g_h_low = g_h.astype(BF)
    g_hb = gather_tp(g_h_low)
    ffn_sum.run(meanwhile=(g_h_low,))
    ffn_sum.run(meanwhile=(g_h_low,))
    g_hb = after(g_hb, *ffn_sum.run())

    g_mixed = nt(g_hb, w_out).astype(BF)
    g_query, *g_kv_far = call_far_back(bias, edges, start_row, q_rot, g_mixed, kv_far)
    arrived = [shift(g, -s) for s, g in zip(range(1, n_ctx), g_kv_far)]
    g_query, g_kv = call_own_back(bias, edges, start_row, q_rot, g_mixed, kv_own, g_query)
    down = scatter_tp(after(down, g_hb))
    g_kv = after(g_kv, down)
    g_qkv, m1, back = call_qkv_back(
        n_tp, g_query, g_kv, q_rot, kv_own, cos, sin, w_query, w_key, w_value, arrived
    )
    ffn_sum.run(meanwhile=(g_qkv,))
    dn1 = scatter_tp(back)
    m1 = tp.total(m1[0]) / width
    tail = call_tail_grad(order, bits, normed, g_qkv, mixed, g_hb)
    tail_sum = SumCtx(tail, n_ctx, rank)
    for _ in range(4):
        tail_sum.run()
    hid = w_gate.shape[1]
    outs = (h + down.astype(F32)).astype(BF)
    down_sum = ffn_sum.result(0, 2 * hid, per * share)
    grad_down = jnp.concatenate([down_sum[i * hid : (i + 1) * hid] for i in range(n_tp // per)], 1)
    grad_gate, grad_up = ffn_sum.result(0, 0, hid), ffn_sum.result(0, hid, hid)
    dn1, outs, grad_gate, grad_up, grad_down = lax.optimization_barrier(
        (dn1, outs, grad_gate, grad_up, grad_down)
    )
    dn1 = dn1.astype(F32)
    r1 = broad(r1)
    x_hat = layer_in.astype(F32) * r1
    g_input = g_h + r1 * (dn1 * gain_a_own - x_hat * m1[:, None])
    grad_gain_one = jnp.sum(dn1 * x_hat, axis=0)
    gains = jnp.concatenate([grad_gain_one, grad_gain_two])
    gains = sum(
        [lax.ppermute(gains, "ctx", [(r, (r + s) % n_ctx) for r in range(n_ctx)]) for s in range(1, n_ctx)],
        gains,
    )
    return (
        outs,
        g_input,
        gains[:share],
        gains[share:],
        tail_sum.result(0, 0, HDIM),
        tail_sum.result(0, HDIM, HDIM),
        tail_sum.result(0, 2 * HDIM, HDIM),
        tail_sum.result(0, 3 * HDIM, HDIM).T,
        grad_gate,
        grad_up,
        grad_down,
    )


def solution(mesh):
    row, col = P("tp", None), P(None, "tp")
    both = P("ctx", "tp")
    in_specs = (both, P(), P(), col, col, col, row, col, col, row, P("ctx"), P("ctx"), both)
    out_specs = (both, both, P("tp"), P("tp"), col, col, col, row, col, col, row)
    return jax.shard_map(
        per_device, mesh=mesh, in_specs=in_specs, out_specs=out_specs, check_vma=False
    )
```

```python
import functools
import math

import jax
import jax.numpy as jnp
from jax import lax
from jax.experimental import pallas as pl
from jax.experimental.pallas import tpu as pltpu
from jax.sharding import PartitionSpec as P

HDIM = 128
EPS = 1e-05
THETA = 10000.0
LOG2E = math.log2(math.e)
SCALE = 1.0 / math.sqrt(HDIM)
BF = jnp.bfloat16
F32 = jnp.float32
I32 = jnp.int32
BQ, BK = 512, 512
VMEM_BYTES = 60 * 1024 * 1024
COST = 1.0

SM = pl.BlockSpec(memory_space=pltpu.SMEM)
VM = pl.BlockSpec(memory_space=pltpu.VMEM)


def shape(dims, dtype):
    return jax.ShapeDtypeStruct(dims, dtype)


def params():
    return pltpu.CompilerParams(vmem_limit_bytes=VMEM_BYTES)


def cost(mults, size):
    return pl.CostEstimate(flops=int(2 * mults * COST), bytes_accessed=int(size * COST), transcendentals=0)


def nn(a, b):
    return lax.dot_general(a, b, (((1,), (0,)), ((), ())), preferred_element_type=F32)


def nt(a, b):
    return lax.dot_general(a, b, (((1,), (1,)), ((), ())), preferred_element_type=F32)


def tn(a, b):
    return lax.dot_general(a, b, (((0,), (0,)), ((), ())), preferred_element_type=F32)


def add(a, b):
    return b if a is None else a + b


def tiles(width, k, n=None):
    return pl.ds(pl.multiple_of(k * width, width), width)


def row_sums(a):
    high = a.astype(BF)
    low = (a - high.astype(F32)).astype(BF)
    ones = jnp.ones((8, a.shape[1]), BF)
    return nt(ones, high) + nt(ones, low)


def qkv_kernel(n, order, *refs):
    xs = refs[:n]
    gain, wq, wk, wv, cos, sin, normed, q, kv, r1_out = refs[n:]
    share = xs[0].shape[1]
    squares = None
    for k in range(n):
        v = xs[k][...].astype(F32)
        squares = add(squares, v * v)
    r1 = lax.rsqrt(jnp.sum(squares, axis=-1, keepdims=True) / (n * share) + EPS)
    sums = [None] * 3
    for k in range(n):
        block = (xs[k][...].astype(F32) * r1 * gain[pl.ds(order[k], 1), :]).astype(BF)
        normed[:, k * share : (k + 1) * share] = block
        rows = tiles(share, order[k])
        for i, w in enumerate((wq, wk, wv)):
            sums[i] = add(sums[i], nn(block, w[rows, :]))
    c, s = cos[...], sin[...]

    def rotated(v):
        return v * c + pltpu.roll(v, HDIM // 2, 1) * s

    q[...] = rotated(sums[0]).astype(BF)
    kv[:, :HDIM] = rotated(sums[1]).astype(BF)
    kv[:, HDIM:] = sums[2].astype(BF)
    r1_out[...] = jnp.broadcast_to(r1, r1_out.shape)


def call_qkv(order, xs, gain, wq, wk, wv, cos, sin):
    n = len(xs)
    tok, share = xs[0].shape
    bt = min(tok, 256)

    def row(w):
        return pl.BlockSpec((bt, w), lambda i, o: (i, 0))

    def full(a):
        return pl.BlockSpec(a.shape, lambda i, o: (0, 0))

    spec = pltpu.PrefetchScalarGridSpec(
        num_scalar_prefetch=1,
        grid=(tok // bt,),
        in_specs=[row(share)] * n + [full(a) for a in (gain, wq, wk, wv)] + [row(HDIM)] * 2,
        out_specs=[row(n * share), row(HDIM), row(2 * HDIM), row(128)],
    )
    return pl.pallas_call(
        functools.partial(qkv_kernel, n),
        grid_spec=spec,
        out_shape=[
            shape((tok, n * share), BF),
            shape((tok, HDIM), BF),
            shape((tok, 2 * HDIM), BF),
            shape((tok, 128), F32),
        ],
        compiler_params=params(),
        cost_estimate=cost(5 * tok * n * share * HDIM * 4, 10 * tok * n * share),
        name="norm_qkv",
    )(order, *xs, gain, wq, wk, wv, cos, sin)


def edges_of(rank, tok, starts):
    t = starts.reshape(tok // BQ, BQ)
    return jnp.concatenate([(rank * tok)[None], jnp.stack([t[:, 0], t[:, -1]], axis=1).reshape(-1)])


def sigmoid_of(raw, bias):
    return 1.0 / (1.0 + jnp.exp2(raw * (-LOG2E * SCALE) - bias * LOG2E))


def own_kernel(bias, tok, edges, start, q, kv, total):
    base = edges[0]
    for qi in range(tok // BQ):
        rows = slice(qi * BQ, (qi + 1) * BQ)
        q_tile = q[rows, :]
        first_key = start[rows, :] - base
        q_index = qi * BQ + lax.broadcasted_iota(I32, (BQ, 1), 0)

        def body(ki, acc):
            at = tiles(BK, ki)
            w = sigmoid_of(nt(q_tile, kv[at, :HDIM]), bias)
            k_index = ki * BK + lax.broadcasted_iota(I32, (BQ, BK), 1)
            w = jnp.where((k_index >= first_key) & (k_index <= q_index), w, 0.0)
            return acc + nn(w.astype(BF), kv[at, HDIM:])

        low = jnp.maximum(edges[1 + 2 * qi] - base, 0) // BK
        high = ((qi + 1) * BQ + BK - 1) // BK
        total[rows, :] = lax.fori_loop(low, high, body, jnp.zeros((BQ, HDIM), F32))


def far_kernel(bias, tok, q0, n_far, n, edges, order, start, q, acc, wo, *refs):
    kvs, mixed, pieces = refs[:n_far], refs[n_far], refs[n_far + 1 :]
    share = wo.shape[1] // n
    n_keys = tok // BK
    for qi in range(q.shape[0] // BQ):
        rows = slice(qi * BQ, (qi + 1) * BQ)
        at_first, at_last = 1 + 2 * (q0 // BQ + qi), 2 + 2 * (q0 // BQ + qi)
        q_tile = q[rows, :]
        total = acc[rows, :]
        for i in range(n_far):
            base = edges[0] - (i + 1) * tok
            kv = kvs[i]
            first_key = start[rows, :] - base

            def body(ki, total, masked):
                at = tiles(BK, ki)
                w = sigmoid_of(nt(q_tile, kv[at, :HDIM]), bias)
                if masked:
                    k_index = ki * BK + lax.broadcasted_iota(I32, (BQ, BK), 1)
                    w = jnp.where(k_index >= first_key, w, 0.0)
                return total + nn(w.astype(BF), kv[at, HDIM:])

            low = jnp.clip(edges[at_first] - base, 0, tok) // BK
            mid = jnp.clip(edges[at_last] - base + BK - 1, 0, tok) // BK
            mid = jnp.maximum(low, mid)
            total = lax.fori_loop(low, mid, functools.partial(body, masked=True), total)
            total = lax.fori_loop(mid, n_keys, functools.partial(body, masked=False), total)
        rounded = total.astype(BF)
        mixed[rows, :] = rounded
        for k in range(n):
            pieces[k][rows, :] = nn(rounded, wo[:, tiles(share, order[k])]).astype(BF)


def tile_back(bias, q_tile, g_tile, k_tile, v_tile, keep, g_query, rows, sums):
    s = sigmoid_of(nt(k_tile, q_tile), bias)
    g_weight = nt(v_tile, g_tile)
    if keep is not None:
        s = jnp.where(keep, s, 0.0)
    g_s = (g_weight * (s * (1.0 - s))).astype(BF)
    g_value = sums[1] + nn(s.astype(BF), g_tile)
    g_key = sums[0] + nn(g_s, q_tile)
    g_query[rows, :] = g_query[rows, :] + tn(g_s, k_tile)
    return g_key, g_value


def count_tiles(edges, n_q, which, limit):
    return sum([(edges[which + 2 * i] <= limit).astype(I32) for i in range(n_q)], jnp.int32(0))


def far_back_kernel(bias, tok, n_far, edges, start, q, g, *refs):
    kvs, g_query, outs = refs[:n_far], refs[n_far], refs[n_far + 1 :]
    n_q = tok // BQ
    g_query[...] = jnp.zeros_like(g_query)
    for i in reversed(range(n_far)):
        base = edges[0] - (i + 1) * tok
        kv, out = kvs[i], outs[i]

        def key_tile(ki, carry):
            at = tiles(BK, ki)
            k_tile, v_tile = kv[at, :HDIM], kv[at, HDIM:]
            key0 = base + ki * BK
            high = count_tiles(edges, n_q, 1, key0 + BK - 1)
            mid = count_tiles(edges, n_q, 2, key0)

            def body(qi, sums, masked):
                r = tiles(BQ, qi)
                keep = None
                if masked:
                    keep = key0 + lax.broadcasted_iota(I32, (BK, BQ), 0) >= start[:, r]
                return tile_back(bias, q[r, :], g[r, :], k_tile, v_tile, keep, g_query, r, sums)

            zero = jnp.zeros((BK, HDIM), F32)
            sums = lax.fori_loop(0, mid, functools.partial(body, masked=False), (zero, zero))
            g_key, g_value = lax.fori_loop(mid, high, functools.partial(body, masked=True), sums)
            out[at, :HDIM] = (g_key * SCALE).astype(BF)
            out[at, HDIM:] = g_value.astype(BF)
            return carry

        live = jnp.logical_and(base >= 0, edges[1] <= base + tok - 1)

        @pl.when(live)
        def _():
            lax.fori_loop(0, tok // BK, key_tile, 0)

        @pl.when(jnp.logical_not(live))
        def _():
            out[...] = jnp.zeros_like(out)


def own_back_kernel(bias, tok, edges, start, q, g, kv, g_query_in, g_query, out):
    n_q = tok // BQ
    base = edges[0]
    g_query[...] = g_query_in[...]
    for ki in range(tok // BK):
        at = slice(ki * BK, (ki + 1) * BK)
        k_tile, v_tile = kv[at, :HDIM], kv[at, HDIM:]
        key0 = base + ki * BK

        def body(qi, sums):
            r = tiles(BQ, qi)
            k_index = key0 + lax.broadcasted_iota(I32, (BK, BQ), 0)
            q_index = base + qi * BQ + lax.broadcasted_iota(I32, (1, BQ), 1)
            keep = (k_index >= start[:, r]) & (k_index <= q_index)
            return tile_back(bias, q[r, :], g[r, :], k_tile, v_tile, keep, g_query, r, sums)

        zero = jnp.zeros((BK, HDIM), F32)
        high = count_tiles(edges, n_q, 1, key0 + BK - 1)
        g_key, g_value = lax.fori_loop((ki * BK) // BQ, high, body, (zero, zero))
        out[at, :HDIM] = g_key * SCALE
        out[at, HDIM:] = g_value


def call_own(bias, edges, start, q, kv):
    tok = q.shape[0]
    return pl.pallas_call(
        functools.partial(own_kernel, bias, tok),
        out_shape=shape((tok, HDIM), F32),
        in_specs=[SM, VM, VM, VM],
        out_specs=VM,
        compiler_params=params(),
        cost_estimate=cost(16 * tok * tok * HDIM, 4 * tok * HDIM),
        name="attend_own",
    )(edges, start, q, kv)


def call_far(bias, tok, c, rows, edges, order, start, q, acc, wo, kvs):
    n = order.shape[0]

    def part(w):
        return pl.BlockSpec((rows, w), lambda i: (c, 0))

    def full(a):
        return pl.BlockSpec(a.shape, lambda i: (0, 0))

    out = pl.BlockSpec((rows, HDIM), lambda i: (0, 0))
    share = wo.shape[1] // n
    return pl.pallas_call(
        functools.partial(far_kernel, bias, tok, c * rows, len(kvs), n),
        grid=(1,),
        out_shape=[shape((rows, HDIM), BF)] + [shape((rows, share), BF)] * n,
        in_specs=[SM, SM, part(1), part(HDIM), part(HDIM), full(wo)] + [full(a) for a in kvs],
        out_specs=[out] + [pl.BlockSpec((rows, share), lambda i: (0, 0))] * n,
        compiler_params=params(),
        cost_estimate=cost(20 * rows * tok * HDIM + 12 * rows * n * share * HDIM, 4 * rows * n * share),
        name="attend_far",
    )(edges, order, start, q, acc, wo, *kvs)


def call_far_back(bias, edges, start, q, g, kvs):
    tok = q.shape[0]
    return pl.pallas_call(
        functools.partial(far_back_kernel, bias, tok, len(kvs)),
        out_shape=[shape((tok, HDIM), F32)] + [shape((tok, 2 * HDIM), BF)] * len(kvs),
        in_specs=[SM] + [VM] * (3 + len(kvs)),
        out_specs=[VM] * (1 + len(kvs)),
        compiler_params=params(),
        cost_estimate=cost(48 * tok * tok * HDIM, 16 * tok * HDIM),
        name="attend_far_back",
    )(edges, start, q, g, *kvs)


def call_own_back(bias, edges, start, q, g, kv, g_query):
    tok = q.shape[0]
    return pl.pallas_call(
        functools.partial(own_back_kernel, bias, tok),
        out_shape=[shape((tok, HDIM), F32), shape((tok, 2 * HDIM), F32)],
        in_specs=[SM] + [VM] * 5,
        out_specs=[VM] * 2,
        compiler_params=params(),
        cost_estimate=cost(28 * tok * tok * HDIM, 16 * tok * HDIM),
        name="attend_own_back",
    )(edges, start, q, g, kv, g_query)


def ffn_start_kernel(n, order, *refs):
    hs = refs[:n]
    cot, inv_gain, wg, wu, wd, gate_out, up_out, g_hidden, squares_out = refs[n:]
    share = hs[0].shape[1]
    squares = gate = up = None
    for k in range(n):
        h = hs[k][...]
        v = h.astype(F32) * inv_gain[pl.ds(order[k], 1), :]
        squares = add(squares, v * v)
        rows = tiles(share, order[k])
        gate = add(gate, nn(h, wg[rows, :]))
        up = add(up, nn(h, wu[rows, :]))
    gate_out[...] = gate
    up_out[...] = up
    g_hidden[...] = nt(cot[...], wd[...])
    squares_out[...] = squares


def call_ffn_start(order, hs, cot, inv_gain, wg, wu, wd):
    n, (rows, share) = len(hs), hs[0].shape
    hid = wd.shape[0]
    bt = min(rows, 256)

    def row(w):
        return pl.BlockSpec((bt, w), lambda i, o: (i, 0))

    def full(a):
        return pl.BlockSpec(a.shape, lambda i, o: (0, 0))

    spec = pltpu.PrefetchScalarGridSpec(
        num_scalar_prefetch=1,
        grid=(rows // bt,),
        in_specs=[row(share)] * n + [row(cot.shape[1])] + [full(a) for a in (inv_gain, wg, wu, wd)],
        out_specs=[row(hid)] * 3 + [row(share)],
    )
    return pl.pallas_call(
        functools.partial(ffn_start_kernel, n),
        grid_spec=spec,
        out_shape=[shape((rows, hid), F32)] * 3 + [shape((rows, share), F32)],
        compiler_params=params(),
        cost_estimate=cost(2 * 2 * rows * cot.shape[1] * hid, 14 * rows * cot.shape[1]),
        name="ffn_start",
    )(order, *hs, cot, inv_gain, wg, wu, wd)


def ffn_kernel(n, late, order, *refs):
    hs = refs[: len(late)]
    gate, up, g_hidden, squares, inv_gain, wg, wu, hidden, g_gu, r2_out, m2, back = refs[len(late) :]
    share, hid = hs[0].shape[1], wg.shape[1]
    gate, up, squares, g_hidden = gate[...], up[...], squares[...], g_hidden[...]
    for k, h_ref in zip(late, hs):
        h = h_ref[...]
        v = h.astype(F32) * inv_gain[pl.ds(order[k], 1), :]
        squares = squares + v * v
        rows = tiles(share, order[k])
        gate = gate + nn(h, wg[rows, :])
        up = up + nn(h, wu[rows, :])
    r2 = lax.rsqrt(jnp.sum(squares, axis=-1, keepdims=True) / (n * share) + EPS)
    gate = gate * r2
    up = up * r2
    sig = jax.nn.sigmoid(gate)
    silu = gate * sig
    hidden[...] = (silu * up).astype(BF)
    g_gate = g_hidden * up * sig * (1.0 + gate * (1.0 - sig))
    g_up = g_hidden * silu
    m2[...] = row_sums(g_gate * gate + g_up * up)
    g_gate = (g_gate * r2).astype(BF)
    g_up = (g_up * r2).astype(BF)
    g_gu[:, :hid] = g_gate
    g_gu[:, hid:] = g_up
    r2_out[...] = jnp.broadcast_to(r2, r2_out.shape)
    for k in range(n):
        rows = slice(k * share, (k + 1) * share)
        back[:, rows] = (nt(g_gate, wg[rows, :]) + nt(g_up, wu[rows, :])).astype(BF)


def call_ffn(order, hs, begun, inv_gain, wg, wu):
    n = order.shape[0]
    late = list(range(n - len(hs), n))
    rows, share = hs[0].shape
    hid = wg.shape[1]
    bt = min(rows, 256)

    def row(w):
        return pl.BlockSpec((bt, w), lambda i, o: (i, 0))

    def full(a):
        return pl.BlockSpec(a.shape, lambda i, o: (0, 0))

    spec = pltpu.PrefetchScalarGridSpec(
        num_scalar_prefetch=1,
        grid=(rows // bt,),
        in_specs=[row(share)] * len(hs)
        + [row(hid)] * 3
        + [row(share)]
        + [full(a) for a in (inv_gain, wg, wu)],
        out_specs=[row(hid), row(2 * hid), row(128), pl.BlockSpec((8, bt), lambda i, o: (0, i)), row(n * share)],
    )
    return pl.pallas_call(
        functools.partial(ffn_kernel, n, late),
        grid_spec=spec,
        out_shape=[
            shape((rows, hid), BF),
            shape((rows, 2 * hid), BF),
            shape((rows, 128), F32),
            shape((8, rows), F32),
            shape((rows, n * share), BF),
        ],
        compiler_params=params(),
        cost_estimate=cost(2 * 3 * rows * n * share * hid, 14 * rows * n * share),
        name="ffn",
    )(order, *hs, *begun, inv_gain, wg, wu)


def put(parts, bits, row, rows, cols, value):
    size = parts.shape[1]
    quarter = row // size
    half = quarter // 2
    goes = (quarter % 2 != bits[half]).astype(I32)
    at = pl.ds(pl.multiple_of(row - quarter * size, rows), rows)
    parts[half * 2 + goes, at, cols] = value


def ffn_grad_kernel(n, per, order, bits, cot, *refs):
    lefts, g_gu, hidden, outs, parts = refs[:n], refs[n], refs[n + 1], refs[n + 2 : -1], refs[-1]
    share, wide, hid = lefts[0].shape[1], g_gu.shape[1], hidden.shape[1]
    step = min(hid, parts.shape[1])
    for k in range(n):
        value = tn(lefts[k][...], g_gu[...]).astype(BF)
        put(parts, bits, order[k] * share, share, slice(0, wide), value)
        row, col = (k // per) * hid, wide + (k % per) * share
        value = tn(hidden[...], cot[:, k * share : (k + 1) * share]).astype(BF)
        for r in range(0, hid, step):
            put(parts, bits, jnp.int32(row + r), step, slice(col, col + share), value[r : r + step, :])
    for i, out in enumerate(outs):
        out[...] = parts[i]


def call_ffn_grad(order, bits, per, cot, lefts, g_gu, hidden):
    n = order.shape[0]
    wide = g_gu.shape[1] + per * lefts[0].shape[1]
    return pl.pallas_call(
        functools.partial(ffn_grad_kernel, n, per),
        out_shape=[shape((cot.shape[1] // 4, wide), BF)] * 4,
        in_specs=[SM, SM] + [VM] * (3 + len(lefts)),
        out_specs=[VM] * 4,
        scratch_shapes=[pltpu.VMEM((4, cot.shape[1] // 4, wide), BF)],
        compiler_params=params(),
        cost_estimate=cost(2 * cot.shape[0] * cot.shape[1] * wide, 8 * cot.shape[0] * cot.shape[1]),
        name="grad_ffn",
    )(order, bits, cot, *lefts, g_gu, hidden)


def qkv_back_kernel(n, n_far, g_query, g_kv, q, kv, cos, sin, wq, wk, wv, *refs):
    arrived, (g_qkv, m1, out) = refs[:n_far], refs[n_far:]
    share = wq.shape[0] // n
    total = g_kv[...]
    for a in arrived:
        total = total + a[...].astype(F32)
    gq, gk, gv = g_query[...] * SCALE, total[:, :HDIM], total[:, HDIM:]
    m1[...] = row_sums(
        gq * q[...].astype(F32) + gk * kv[:, :HDIM].astype(F32) + gv * kv[:, HDIM:].astype(F32)
    )
    c, s = cos[...], sin[...]

    def back(v):
        return (v * c - pltpu.roll(v, HDIM // 2, 1) * s).astype(BF)

    gq, gk, gv = back(gq), back(gk), gv.astype(BF)
    g_qkv[:, :HDIM] = gq
    g_qkv[:, HDIM : 2 * HDIM] = gk
    g_qkv[:, 2 * HDIM :] = gv
    for k in range(n):
        rows = slice(k * share, (k + 1) * share)
        out[:, rows] = (nt(gq, wq[rows, :]) + nt(gk, wk[rows, :]) + nt(gv, wv[rows, :])).astype(BF)


def call_qkv_back(n, g_query, g_kv, q, kv, cos, sin, wq, wk, wv, arrived):
    n_far = len(arrived)
    tok = q.shape[0]
    bt = min(tok, 256)

    def row(w):
        return pl.BlockSpec((bt, w), lambda i: (i, 0))

    def full(a):
        return pl.BlockSpec(a.shape, lambda i: (0, 0))

    width = wq.shape[0]
    return pl.pallas_call(
        functools.partial(qkv_back_kernel, n, n_far),
        grid=(tok // bt,),
        in_specs=[row(HDIM), row(2 * HDIM), row(HDIM), row(2 * HDIM), row(HDIM), row(HDIM)]
        + [full(a) for a in (wq, wk, wv)]
        + [row(2 * HDIM)] * n_far,
        out_specs=[row(3 * HDIM), pl.BlockSpec((8, bt), lambda i: (0, i)), row(width)],
        out_shape=[shape((tok, 3 * HDIM), BF), shape((8, tok), F32), shape((tok, width), BF)],
        compiler_params=params(),
        cost_estimate=cost(6 * tok * width * 3 * HDIM, 4 * tok * width),
        name="qkv_back",
    )(g_query, g_kv, q, kv, cos, sin, wq, wk, wv, *arrived)


def tail_grad_kernel(n, order, bits, left, g_qkv, mixed, g_hb, *refs):
    outs, parts = refs[:-1], refs[-1]
    share = left.shape[1] // n
    for k in range(n):
        block = slice(k * share, (k + 1) * share)
        value = tn(left[:, block], g_qkv[...]).astype(BF)
        put(parts, bits, order[k] * share, share, slice(0, 3 * HDIM), value)
        value = tn(g_hb[:, block], mixed[...]).astype(BF)
        put(parts, bits, jnp.int32(k * share), share, slice(3 * HDIM, 4 * HDIM), value)
    for i, out in enumerate(outs):
        out[...] = parts[i]


def call_tail_grad(order, bits, left, g_qkv, mixed, g_hb):
    return pl.pallas_call(
        functools.partial(tail_grad_kernel, order.shape[0]),
        out_shape=[shape((left.shape[1] // 4, 4 * HDIM), BF)] * 4,
        in_specs=[SM, SM] + [VM] * 4,
        out_specs=[VM] * 4,
        scratch_shapes=[pltpu.VMEM((4, left.shape[1] // 4, 4 * HDIM), BF)],
        compiler_params=params(),
        cost_estimate=cost(4 * left.shape[0] * left.shape[1] * 4 * HDIM, 4 * left.shape[0] * left.shape[1]),
        name="grad_tail",
    )(order, bits, left, g_qkv, mixed, g_hb)


def folded(n):
    return [0] + list(range(1, n, 2)) + list(range(n - 2 + n % 2, 0, -2))


class Tp:
    def __init__(self, n_tp):
        self.n = n_tp
        self.pairs = n_tp // 2
        ring = folded(self.pairs)
        place = [ring.index(z) for z in range(self.pairs)]
        self.core_perm = [(i, i ^ 1) for i in range(n_tp)]
        self.ring_to = []
        order = []
        for i in range(n_tp):
            z, c = divmod(i, 2)
            self.ring_to.append(ring[(place[z] + 1) % self.pairs] * 2 + c)
            sources = [ring[(place[z] - j) % self.pairs] * 2 for j in range(self.pairs)]
            order.append([s + (c ^ b) for s in sources for b in (0, 1)])
        self.order = jnp.asarray(order, I32)[lax.axis_index("tp")]

    def core(self, a):
        return lax.ppermute(a, "tp", self.core_perm)

    def step(self, a, distance=1):
        perm = []
        for i in range(self.n):
            j = i
            for _ in range(distance):
                j = self.ring_to[j]
            perm.append((i, j))
        return lax.ppermute(a, "tp", perm)

    def gather(self, block, gates=None, beside=None):
        got, cur = [], block
        for j in range(self.pairs):
            if gates and j in gates:
                cur = after(cur, *gates[j](cur))
            if j:
                cur = self.step(cur)
            if beside and j == self.pairs - 1:
                extra = beside(got)
                cur = after(cur, *extra)
            got += [cur, self.core(cur)]
        return (got, extra) if beside else got

    def scatter(self, pieces):
        acc = None
        for j in list(range(1, self.pairs)) + [0]:
            term = pieces[2 * j].astype(F32) + self.core(pieces[2 * j + 1]).astype(F32)
            if acc is not None:
                term = term + self.step(acc.astype(BF)).astype(F32)
            acc = term
        return acc

    def total(self, small):
        small = small + self.core(small)
        return sum([self.step(small, d) for d in range(1, self.pairs)], small)


def scatter_tp(a):
    return lax.psum_scatter(a, "tp", scatter_dimension=1, tiled=True)


def gather_tp(a):
    return lax.all_gather(a, "tp", axis=1, tiled=True)


def after(value, *others):
    return lax.optimization_barrier((value, *others))[0]


class SumCtx:
    def __init__(self, quarters, n_ctx, rank):
        self.n, self.bits = n_ctx, (rank % 2, rank // 2)
        self.quarters = quarters
        self.parts = [None, None] if n_ctx == 4 else [jnp.concatenate(quarters, 0)]
        self.phase = 0
        self.arrived = []

    def send(self):
        if self.n == 4:
            self.arrived = [self.swap(self.quarters[2 * i + 1], i) for i in (0, 1)]
        return self.arrived

    def swap(self, a, axis):
        return lax.ppermute(a, "ctx", [(r, r ^ (1 << axis)) for r in range(4)])

    def run(self, before=(), meanwhile=()):
        phase = self.phase
        self.phase += 1
        parts = [after(p, *before) for p in self.parts] if before else self.parts
        if self.n != 4:
            if phase == 0:
                self.parts = list(lax.psum(tuple(parts), "ctx"))
            return self.parts
        self.parts = []
        self.last = []
        for i, part in enumerate(parts):
            axis = (i + phase) % 2 if phase < 2 else (i + 1 + phase) % 2
            bit = self.bits[axis]
            give = part
            if phase == 0:
                part, give = self.quarters[2 * i : 2 * i + 2]
            elif phase == 1:
                half = part.shape[0] // 2
                give = lax.dynamic_slice_in_dim(part, (1 - bit) * half, half, 0)
                part = lax.dynamic_slice_in_dim(part, bit * half, half, 0)
            got = self.arrived[i] if phase == 0 and self.arrived else self.swap(give, axis)
            if meanwhile:
                got = after(got, *meanwhile)
            self.last.append((bit, part, got))
            if phase < 2:
                self.parts.append((part.astype(F32) + got.astype(F32)).astype(BF))
            elif phase == 2:
                self.parts.append(self.joined(bit, part, got))
        return self.parts or [got for _, _, got in self.last]

    def hold(self, gate):
        if self.n == 4:
            self.last = [(bit, part, after(got, gate)) for bit, part, got in self.last]

    def joined(self, bit, part, got):
        return jnp.where(bit == 0, jnp.concatenate([part, got], 0), jnp.concatenate([got, part], 0))

    def result(self, at, first=None, width=None):
        take = slice(None) if first is None else slice(first, first + width)
        if self.n != 4:
            return self.parts[at][:, take].astype(F32)
        both = [self.joined(bit, part[:, take], got[:, take]) for bit, part, got in self.last[2 * at : 2 * at + 2]]
        return jnp.concatenate(both, 0).astype(F32)


def per_device(
    layer_in,
    gain_attn,
    gain_ffn,
    w_query,
    w_key,
    w_value,
    w_out,
    w_gate,
    w_up,
    w_down,
    doc_ids,
    positions,
    cotangent,
):
    tok, share = layer_in.shape
    n_ctx, n_tp = lax.axis_size("ctx"), lax.axis_size("tp")
    width = share * n_tp
    tp = Tp(n_tp)
    order = tp.order
    rank = lax.axis_index("ctx").astype(I32)
    own = lax.axis_index("tp") * share
    bias = -math.log(tok * n_ctx)
    per = max(1, min(4 * HDIM // share, n_tp))
    bits = jnp.stack([rank % 2, rank // 2]) if n_ctx == 4 else jnp.zeros((2,), I32)
    gain_a_own = lax.dynamic_slice_in_dim(gain_attn, own, share, 0)
    gain_f_own = lax.dynamic_slice_in_dim(gain_ffn, own, share, 0)

    def shift(a, s):
        return lax.ppermute(a, "ctx", [(r, r + s) for r in range(n_ctx) if 0 <= r + s < n_ctx])

    def broad(a):
        return jnp.tile(a, (1, share // a.shape[1]))

    freq = THETA ** (-(jnp.arange(HDIM // 2, dtype=F32) * 2.0 / HDIM))
    angle = positions.astype(F32)[:, None] * freq[None, :]
    cos, sin = jnp.cos(angle), jnp.sin(angle)
    cos, sin = jnp.concatenate([cos, cos], 1), jnp.concatenate([-sin, sin], 1)
    q_start = rank * tok + jnp.arange(tok, dtype=I32) - positions
    edges = edges_of(rank, tok, q_start)
    gain_blocks, inv_gain = gain_attn.reshape(n_tp, share), (1.0 / gain_ffn).reshape(n_tp, share)
    start_col, start_row = q_start[:, None], q_start[None, :]
    prepared = lax.optimization_barrier((cos, sin, edges, start_col, start_row, gain_blocks, inv_gain, order))
    cos, sin, edges, start_col, start_row, gain_blocks, inv_gain, order = prepared
    xs = tp.gather(layer_in, {2: lambda arrived: prepared})
    normed, q_rot, kv_own, r1 = call_qkv(order, xs, gain_blocks, w_query, w_key, w_value, cos, sin)
    cot_full = lax.all_gather(after(cotangent, xs[-2]), "tp", axis=1, tiled=True)
    kv_far = [shift(kv_own, s) for s in range(1, n_ctx)]
    acc = call_own(bias, edges, start_col, q_rot, kv_own)
    mixed, *pieces = call_far(bias, tok, 0, tok, edges, order, start_col, q_rot, acc, w_out, kv_far)
    h = layer_in.astype(F32) + tp.scatter(pieces)
    hs, begun = tp.gather(
        (h * gain_f_own).astype(BF),
        beside=lambda got: call_ffn_start(order, got, cot_full, inv_gain, w_gate, w_up, w_down),
    )

    hidden, g_gu, r2, m2, back = call_ffn(order, hs[-2:], begun, inv_gain, w_gate, w_up)
    dn2 = scatter_tp(back)
    m2 = tp.total(m2[0]) / width
    grad_ffn = call_ffn_grad(order, bits, per, cot_full, hs, g_gu, hidden)
    ffn_sum = SumCtx(grad_ffn, n_ctx, rank)
    down = nn(hidden, after(w_down, grad_ffn[1])).astype(BF)
    dn2 = after(dn2, down, *ffn_sum.send()).astype(F32)
    r2 = broad(r2)
    g_h = cotangent.astype(F32) + gain_f_own * dn2 - (r2 * r2 * m2[:, None]) * h
    grad_gain_two = jnp.sum(dn2 * h, axis=0)
    g_h_low = g_h.astype(BF)
    g_hb = gather_tp(g_h_low)
    ffn_sum.run(meanwhile=(g_h_low,))
    ffn_sum.run(meanwhile=(g_h_low,))
    g_hb = after(g_hb, *ffn_sum.run())

    g_mixed = nt(g_hb, w_out).astype(BF)
    g_query, *g_kv_far = call_far_back(bias, edges, start_row, q_rot, g_mixed, kv_far)
    arrived = [shift(g, -s) for s, g in zip(range(1, n_ctx), g_kv_far)]
    g_query, g_kv = call_own_back(bias, edges, start_row, q_rot, g_mixed, kv_own, g_query)
    down = scatter_tp(after(down, g_hb))
    g_kv = after(g_kv, down, *ffn_sum.run(meanwhile=(g_kv,)))
    g_qkv, m1, back = call_qkv_back(
        n_tp, g_query, g_kv, q_rot, kv_own, cos, sin, w_query, w_key, w_value, arrived
    )
    dn1 = scatter_tp(back)
    m1 = tp.total(m1[0]) / width
    tail = call_tail_grad(order, bits, normed, g_qkv, mixed, g_hb)
    tail_sum = SumCtx(tail, n_ctx, rank)
    for _ in range(3):
        tail_sum.run()
    hid = w_gate.shape[1]
    ffn_sum.hold(tail[1])
    outs = (h + down.astype(F32)).astype(BF)
    down_sum = ffn_sum.result(0, 2 * hid, per * share)
    grad_down = jnp.concatenate([down_sum[i * hid : (i + 1) * hid] for i in range(n_tp // per)], 1)
    grad_gate, grad_up = ffn_sum.result(0, 0, hid), ffn_sum.result(0, hid, hid)
    dn1, outs, grad_gate, grad_up, grad_down = lax.optimization_barrier(
        (dn1, outs, grad_gate, grad_up, grad_down)
    )
    dn1 = dn1.astype(F32)
    r1 = broad(r1)
    x_hat = layer_in.astype(F32) * r1
    g_input = g_h + r1 * (dn1 * gain_a_own - x_hat * m1[:, None])
    grad_gain_one = jnp.sum(dn1 * x_hat, axis=0)
    tail_sum.run(meanwhile=(grad_gain_one,))
    gains = jnp.concatenate([grad_gain_one, grad_gain_two])
    gains = sum(
        [lax.ppermute(gains, "ctx", [(r, (r + s) % n_ctx) for r in range(n_ctx)]) for s in range(1, n_ctx)],
        gains,
    )
    return (
        outs,
        g_input,
        gains[:share],
        gains[share:],
        tail_sum.result(0, 0, HDIM),
        tail_sum.result(0, HDIM, HDIM),
        tail_sum.result(0, 2 * HDIM, HDIM),
        tail_sum.result(0, 3 * HDIM, HDIM).T,
        grad_gate,
        grad_up,
        grad_down,
    )


def solution(mesh):
    row, col = P("tp", None), P(None, "tp")
    both = P("ctx", "tp")
    in_specs = (both, P(), P(), col, col, col, row, col, col, row, P("ctx"), P("ctx"), both)
    out_specs = (both, both, P("tp"), P("tp"), col, col, col, row, col, col, row)
    return jax.shard_map(
        per_device, mesh=mesh, in_specs=in_specs, out_specs=out_specs, check_vma=False
    )
```

```python
import functools
import math

import jax
import jax.numpy as jnp
from jax import lax
from jax.experimental import pallas as pl
from jax.experimental.pallas import tpu as pltpu
from jax.sharding import PartitionSpec as P

HDIM = 128
EPS = 1e-05
THETA = 10000.0
LOG2E = math.log2(math.e)
SCALE = 1.0 / math.sqrt(HDIM)
BF = jnp.bfloat16
F32 = jnp.float32
I32 = jnp.int32
BQ, BK = 512, 512
VMEM_BYTES = 60 * 1024 * 1024
COST = 1.0

SM = pl.BlockSpec(memory_space=pltpu.SMEM)
VM = pl.BlockSpec(memory_space=pltpu.VMEM)


def shape(dims, dtype):
    return jax.ShapeDtypeStruct(dims, dtype)


def params():
    return pltpu.CompilerParams(vmem_limit_bytes=VMEM_BYTES)


def cost(mults, size):
    return pl.CostEstimate(flops=int(2 * mults * COST), bytes_accessed=int(size * COST), transcendentals=0)


def nn(a, b):
    return lax.dot_general(a, b, (((1,), (0,)), ((), ())), preferred_element_type=F32)


def nt(a, b):
    return lax.dot_general(a, b, (((1,), (1,)), ((), ())), preferred_element_type=F32)


def tn(a, b):
    return lax.dot_general(a, b, (((0,), (0,)), ((), ())), preferred_element_type=F32)


def add(a, b):
    return b if a is None else a + b


def tiles(width, k, n=None):
    return pl.ds(pl.multiple_of(k * width, width), width)


def row_sums(a):
    high = a.astype(BF)
    low = (a - high.astype(F32)).astype(BF)
    ones = jnp.ones((8, a.shape[1]), BF)
    return nt(ones, high) + nt(ones, low)


def qkv_kernel(n, order, *refs):
    xs = refs[:n]
    gain, wq, wk, wv, cos, sin, normed, q, kv, r1_out = refs[n:]
    share = xs[0].shape[1]
    squares = None
    for k in range(n):
        v = xs[k][...].astype(F32)
        squares = add(squares, v * v)
    r1 = lax.rsqrt(jnp.sum(squares, axis=-1, keepdims=True) / (n * share) + EPS)
    sums = [None] * 3
    for k in range(n):
        block = (xs[k][...].astype(F32) * r1 * gain[pl.ds(order[k], 1), :]).astype(BF)
        normed[:, k * share : (k + 1) * share] = block
        rows = tiles(share, order[k])
        for i, w in enumerate((wq, wk, wv)):
            sums[i] = add(sums[i], nn(block, w[rows, :]))
    c, s = cos[...], sin[...]

    def rotated(v):
        return v * c + pltpu.roll(v, HDIM // 2, 1) * s

    q[...] = rotated(sums[0]).astype(BF)
    kv[:, :HDIM] = rotated(sums[1]).astype(BF)
    kv[:, HDIM:] = sums[2].astype(BF)
    r1_out[...] = jnp.broadcast_to(r1, r1_out.shape)


def call_qkv(order, xs, gain, wq, wk, wv, cos, sin):
    n = len(xs)
    tok, share = xs[0].shape
    bt = min(tok, 256)

    def row(w):
        return pl.BlockSpec((bt, w), lambda i, o: (i, 0))

    def full(a):
        return pl.BlockSpec(a.shape, lambda i, o: (0, 0))

    spec = pltpu.PrefetchScalarGridSpec(
        num_scalar_prefetch=1,
        grid=(tok // bt,),
        in_specs=[row(share)] * n + [full(a) for a in (gain, wq, wk, wv)] + [row(HDIM)] * 2,
        out_specs=[row(n * share), row(HDIM), row(2 * HDIM), row(128)],
    )
    return pl.pallas_call(
        functools.partial(qkv_kernel, n),
        grid_spec=spec,
        out_shape=[
            shape((tok, n * share), BF),
            shape((tok, HDIM), BF),
            shape((tok, 2 * HDIM), BF),
            shape((tok, 128), F32),
        ],
        compiler_params=params(),
        cost_estimate=cost(5 * tok * n * share * HDIM * 4, 10 * tok * n * share),
        name="norm_qkv",
    )(order, *xs, gain, wq, wk, wv, cos, sin)


def edges_of(rank, tok, starts):
    t = starts.reshape(tok // BQ, BQ)
    return jnp.concatenate([(rank * tok)[None], jnp.stack([t[:, 0], t[:, -1]], axis=1).reshape(-1)])


def sigmoid_of(raw, bias):
    return 1.0 / (1.0 + jnp.exp2(raw * (-LOG2E * SCALE) - bias * LOG2E))


def own_kernel(bias, tok, edges, start, q, kv, total):
    base = edges[0]
    for qi in range(tok // BQ):
        rows = slice(qi * BQ, (qi + 1) * BQ)
        q_tile = q[rows, :]
        first_key = start[rows, :] - base
        q_index = qi * BQ + lax.broadcasted_iota(I32, (BQ, 1), 0)

        def body(ki, acc):
            at = tiles(BK, ki)
            w = sigmoid_of(nt(q_tile, kv[at, :HDIM]), bias)
            k_index = ki * BK + lax.broadcasted_iota(I32, (BQ, BK), 1)
            w = jnp.where((k_index >= first_key) & (k_index <= q_index), w, 0.0)
            return acc + nn(w.astype(BF), kv[at, HDIM:])

        low = jnp.maximum(edges[1 + 2 * qi] - base, 0) // BK
        high = ((qi + 1) * BQ + BK - 1) // BK
        total[rows, :] = lax.fori_loop(low, high, body, jnp.zeros((BQ, HDIM), F32))


def far_kernel(bias, tok, q0, n_far, n, edges, order, start, q, acc, wo, *refs):
    kvs, mixed, pieces = refs[:n_far], refs[n_far], refs[n_far + 1 :]
    share = wo.shape[1] // n
    n_keys = tok // BK
    for qi in range(q.shape[0] // BQ):
        rows = slice(qi * BQ, (qi + 1) * BQ)
        at_first, at_last = 1 + 2 * (q0 // BQ + qi), 2 + 2 * (q0 // BQ + qi)
        q_tile = q[rows, :]
        total = acc[rows, :]
        for i in range(n_far):
            base = edges[0] - (i + 1) * tok
            kv = kvs[i]
            first_key = start[rows, :] - base

            def body(ki, total, masked):
                at = tiles(BK, ki)
                w = sigmoid_of(nt(q_tile, kv[at, :HDIM]), bias)
                if masked:
                    k_index = ki * BK + lax.broadcasted_iota(I32, (BQ, BK), 1)
                    w = jnp.where(k_index >= first_key, w, 0.0)
                return total + nn(w.astype(BF), kv[at, HDIM:])

            low = jnp.clip(edges[at_first] - base, 0, tok) // BK
            mid = jnp.clip(edges[at_last] - base + BK - 1, 0, tok) // BK
            mid = jnp.maximum(low, mid)
            total = lax.fori_loop(low, mid, functools.partial(body, masked=True), total)
            total = lax.fori_loop(mid, n_keys, functools.partial(body, masked=False), total)
        rounded = total.astype(BF)
        mixed[rows, :] = rounded
        for k in range(n):
            pieces[k][rows, :] = nn(rounded, wo[:, tiles(share, order[k])]).astype(BF)


def tile_back(bias, q_tile, g_tile, k_tile, v_tile, keep, g_query, rows, sums):
    s = sigmoid_of(nt(k_tile, q_tile), bias)
    g_weight = nt(v_tile, g_tile)
    if keep is not None:
        s = jnp.where(keep, s, 0.0)
    g_s = (g_weight * (s * (1.0 - s))).astype(BF)
    g_value = sums[1] + nn(s.astype(BF), g_tile)
    g_key = sums[0] + nn(g_s, q_tile)
    g_query[rows, :] = g_query[rows, :] + tn(g_s, k_tile)
    return g_key, g_value


def count_tiles(edges, n_q, which, limit):
    return sum([(edges[which + 2 * i] <= limit).astype(I32) for i in range(n_q)], jnp.int32(0))


def far_back_kernel(bias, tok, n_far, edges, start, q, g, *refs):
    kvs, g_query, outs = refs[:n_far], refs[n_far], refs[n_far + 1 :]
    n_q = tok // BQ
    g_query[...] = jnp.zeros_like(g_query)
    for i in reversed(range(n_far)):
        base = edges[0] - (i + 1) * tok
        kv, out = kvs[i], outs[i]

        def key_tile(ki, carry):
            at = tiles(BK, ki)
            k_tile, v_tile = kv[at, :HDIM], kv[at, HDIM:]
            key0 = base + ki * BK
            high = count_tiles(edges, n_q, 1, key0 + BK - 1)
            mid = count_tiles(edges, n_q, 2, key0)

            def body(qi, sums, masked):
                r = tiles(BQ, qi)
                keep = None
                if masked:
                    keep = key0 + lax.broadcasted_iota(I32, (BK, BQ), 0) >= start[:, r]
                return tile_back(bias, q[r, :], g[r, :], k_tile, v_tile, keep, g_query, r, sums)

            zero = jnp.zeros((BK, HDIM), F32)
            sums = lax.fori_loop(0, mid, functools.partial(body, masked=False), (zero, zero))
            g_key, g_value = lax.fori_loop(mid, high, functools.partial(body, masked=True), sums)
            out[at, :HDIM] = (g_key * SCALE).astype(BF)
            out[at, HDIM:] = g_value.astype(BF)
            return carry

        live = jnp.logical_and(base >= 0, edges[1] <= base + tok - 1)

        @pl.when(live)
        def _():
            lax.fori_loop(0, tok // BK, key_tile, 0)

        @pl.when(jnp.logical_not(live))
        def _():
            out[...] = jnp.zeros_like(out)


def own_back_kernel(bias, tok, edges, start, q, g, kv, g_query_in, g_query, out):
    n_q = tok // BQ
    base = edges[0]
    g_query[...] = g_query_in[...]
    for ki in range(tok // BK):
        at = slice(ki * BK, (ki + 1) * BK)
        k_tile, v_tile = kv[at, :HDIM], kv[at, HDIM:]
        key0 = base + ki * BK

        def body(qi, sums):
            r = tiles(BQ, qi)
            k_index = key0 + lax.broadcasted_iota(I32, (BK, BQ), 0)
            q_index = base + qi * BQ + lax.broadcasted_iota(I32, (1, BQ), 1)
            keep = (k_index >= start[:, r]) & (k_index <= q_index)
            return tile_back(bias, q[r, :], g[r, :], k_tile, v_tile, keep, g_query, r, sums)

        zero = jnp.zeros((BK, HDIM), F32)
        high = count_tiles(edges, n_q, 1, key0 + BK - 1)
        g_key, g_value = lax.fori_loop((ki * BK) // BQ, high, body, (zero, zero))
        out[at, :HDIM] = g_key * SCALE
        out[at, HDIM:] = g_value


def call_own(bias, edges, start, q, kv):
    tok = q.shape[0]
    return pl.pallas_call(
        functools.partial(own_kernel, bias, tok),
        out_shape=shape((tok, HDIM), F32),
        in_specs=[SM, VM, VM, VM],
        out_specs=VM,
        compiler_params=params(),
        cost_estimate=cost(16 * tok * tok * HDIM, 4 * tok * HDIM),
        name="attend_own",
    )(edges, start, q, kv)


def call_far(bias, tok, c, rows, edges, order, start, q, acc, wo, kvs):
    n = order.shape[0]

    def part(w):
        return pl.BlockSpec((rows, w), lambda i: (c, 0))

    def full(a):
        return pl.BlockSpec(a.shape, lambda i: (0, 0))

    out = pl.BlockSpec((rows, HDIM), lambda i: (0, 0))
    share = wo.shape[1] // n
    return pl.pallas_call(
        functools.partial(far_kernel, bias, tok, c * rows, len(kvs), n),
        grid=(1,),
        out_shape=[shape((rows, HDIM), BF)] + [shape((rows, share), BF)] * n,
        in_specs=[SM, SM, part(1), part(HDIM), part(HDIM), full(wo)] + [full(a) for a in kvs],
        out_specs=[out] + [pl.BlockSpec((rows, share), lambda i: (0, 0))] * n,
        compiler_params=params(),
        cost_estimate=cost(20 * rows * tok * HDIM + 12 * rows * n * share * HDIM, 4 * rows * n * share),
        name="attend_far",
    )(edges, order, start, q, acc, wo, *kvs)


def call_far_back(bias, edges, start, q, g, kvs):
    tok = q.shape[0]
    return pl.pallas_call(
        functools.partial(far_back_kernel, bias, tok, len(kvs)),
        out_shape=[shape((tok, HDIM), F32)] + [shape((tok, 2 * HDIM), BF)] * len(kvs),
        in_specs=[SM] + [VM] * (3 + len(kvs)),
        out_specs=[VM] * (1 + len(kvs)),
        compiler_params=params(),
        cost_estimate=cost(48 * tok * tok * HDIM, 16 * tok * HDIM),
        name="attend_far_back",
    )(edges, start, q, g, *kvs)


def call_own_back(bias, edges, start, q, g, kv, g_query):
    tok = q.shape[0]
    return pl.pallas_call(
        functools.partial(own_back_kernel, bias, tok),
        out_shape=[shape((tok, HDIM), F32), shape((tok, 2 * HDIM), F32)],
        in_specs=[SM] + [VM] * 5,
        out_specs=[VM] * 2,
        compiler_params=params(),
        cost_estimate=cost(28 * tok * tok * HDIM, 16 * tok * HDIM),
        name="attend_own_back",
    )(edges, start, q, g, kv, g_query)


def ffn_start_kernel(n, order, *refs):
    hs = refs[:n]
    cot, inv_gain, wg, wu, wd, gate_out, up_out, g_hidden, squares_out = refs[n:]
    share = hs[0].shape[1]
    squares = gate = up = None
    for k in range(n):
        h = hs[k][...]
        v = h.astype(F32) * inv_gain[pl.ds(order[k], 1), :]
        squares = add(squares, v * v)
        rows = tiles(share, order[k])
        gate = add(gate, nn(h, wg[rows, :]))
        up = add(up, nn(h, wu[rows, :]))
    gate_out[...] = gate
    up_out[...] = up
    g_hidden[...] = nt(cot[...], wd[...])
    squares_out[...] = squares


def call_ffn_start(order, hs, cot, inv_gain, wg, wu, wd):
    n, (rows, share) = len(hs), hs[0].shape
    hid = wd.shape[0]
    bt = min(rows, 256)

    def row(w):
        return pl.BlockSpec((bt, w), lambda i, o: (i, 0))

    def full(a):
        return pl.BlockSpec(a.shape, lambda i, o: (0, 0))

    spec = pltpu.PrefetchScalarGridSpec(
        num_scalar_prefetch=1,
        grid=(rows // bt,),
        in_specs=[row(share)] * n + [row(cot.shape[1])] + [full(a) for a in (inv_gain, wg, wu, wd)],
        out_specs=[row(hid)] * 3 + [row(share)],
    )
    return pl.pallas_call(
        functools.partial(ffn_start_kernel, n),
        grid_spec=spec,
        out_shape=[shape((rows, hid), F32)] * 3 + [shape((rows, share), F32)],
        compiler_params=params(),
        cost_estimate=cost(2 * 2 * rows * cot.shape[1] * hid, 14 * rows * cot.shape[1]),
        name="ffn_start",
    )(order, *hs, cot, inv_gain, wg, wu, wd)


def ffn_kernel(n, late, order, *refs):
    hs = refs[: len(late)]
    gate, up, g_hidden, squares, inv_gain, wg, wu, hidden, g_gu, r2_out, m2, back = refs[len(late) :]
    share, hid = hs[0].shape[1], wg.shape[1]
    gate, up, squares, g_hidden = gate[...], up[...], squares[...], g_hidden[...]
    for k, h_ref in zip(late, hs):
        h = h_ref[...]
        v = h.astype(F32) * inv_gain[pl.ds(order[k], 1), :]
        squares = squares + v * v
        rows = tiles(share, order[k])
        gate = gate + nn(h, wg[rows, :])
        up = up + nn(h, wu[rows, :])
    r2 = lax.rsqrt(jnp.sum(squares, axis=-1, keepdims=True) / (n * share) + EPS)
    gate = gate * r2
    up = up * r2
    sig = jax.nn.sigmoid(gate)
    silu = gate * sig
    hidden[...] = (silu * up).astype(BF)
    g_gate = g_hidden * up * sig * (1.0 + gate * (1.0 - sig))
    g_up = g_hidden * silu
    m2[...] = row_sums(g_gate * gate + g_up * up)
    g_gate = (g_gate * r2).astype(BF)
    g_up = (g_up * r2).astype(BF)
    g_gu[:, :hid] = g_gate
    g_gu[:, hid:] = g_up
    r2_out[...] = jnp.broadcast_to(r2, r2_out.shape)
    for k in range(n):
        rows = slice(k * share, (k + 1) * share)
        back[:, rows] = (nt(g_gate, wg[rows, :]) + nt(g_up, wu[rows, :])).astype(BF)


def call_ffn(order, hs, begun, inv_gain, wg, wu):
    n = order.shape[0]
    late = list(range(n - len(hs), n))
    rows, share = hs[0].shape
    hid = wg.shape[1]
    bt = min(rows, 256)

    def row(w):
        return pl.BlockSpec((bt, w), lambda i, o: (i, 0))

    def full(a):
        return pl.BlockSpec(a.shape, lambda i, o: (0, 0))

    spec = pltpu.PrefetchScalarGridSpec(
        num_scalar_prefetch=1,
        grid=(rows // bt,),
        in_specs=[row(share)] * len(hs)
        + [row(hid)] * 3
        + [row(share)]
        + [full(a) for a in (inv_gain, wg, wu)],
        out_specs=[row(hid), row(2 * hid), row(128), pl.BlockSpec((8, bt), lambda i, o: (0, i)), row(n * share)],
    )
    return pl.pallas_call(
        functools.partial(ffn_kernel, n, late),
        grid_spec=spec,
        out_shape=[
            shape((rows, hid), BF),
            shape((rows, 2 * hid), BF),
            shape((rows, 128), F32),
            shape((8, rows), F32),
            shape((rows, n * share), BF),
        ],
        compiler_params=params(),
        cost_estimate=cost(2 * 3 * rows * n * share * hid, 14 * rows * n * share),
        name="ffn",
    )(order, *hs, *begun, inv_gain, wg, wu)


def put(parts, bits, row, rows, cols, value):
    size = parts.shape[1]
    quarter = row // size
    half = quarter // 2
    goes = (quarter % 2 != bits[half]).astype(I32)
    at = pl.ds(pl.multiple_of(row - quarter * size, rows), rows)
    parts[half * 2 + goes, at, cols] = value


def ffn_grad_kernel(n, per, order, bits, cot, *refs):
    lefts, g_gu, hidden, outs, parts = refs[:n], refs[n], refs[n + 1], refs[n + 2 : -1], refs[-1]
    share, wide, hid = lefts[0].shape[1], g_gu.shape[1], hidden.shape[1]
    step = min(hid, parts.shape[1])
    for k in range(n):
        value = tn(lefts[k][...], g_gu[...]).astype(BF)
        put(parts, bits, order[k] * share, share, slice(0, wide), value)
        row, col = (k // per) * hid, wide + (k % per) * share
        value = tn(hidden[...], cot[:, k * share : (k + 1) * share]).astype(BF)
        for r in range(0, hid, step):
            put(parts, bits, jnp.int32(row + r), step, slice(col, col + share), value[r : r + step, :])
    for i, out in enumerate(outs):
        out[...] = parts[i]


def call_ffn_grad(order, bits, per, cot, lefts, g_gu, hidden):
    n = order.shape[0]
    wide = g_gu.shape[1] + per * lefts[0].shape[1]
    return pl.pallas_call(
        functools.partial(ffn_grad_kernel, n, per),
        out_shape=[shape((cot.shape[1] // 4, wide), BF)] * 4,
        in_specs=[SM, SM] + [VM] * (3 + len(lefts)),
        out_specs=[VM] * 4,
        scratch_shapes=[pltpu.VMEM((4, cot.shape[1] // 4, wide), BF)],
        compiler_params=params(),
        cost_estimate=cost(2 * cot.shape[0] * cot.shape[1] * wide, 8 * cot.shape[0] * cot.shape[1]),
        name="grad_ffn",
    )(order, bits, cot, *lefts, g_gu, hidden)


def qkv_back_kernel(n, n_far, g_query, g_kv, q, kv, cos, sin, wq, wk, wv, *refs):
    arrived, (g_qkv, m1, out) = refs[:n_far], refs[n_far:]
    share = wq.shape[0] // n
    total = g_kv[...]
    for a in arrived:
        total = total + a[...].astype(F32)
    gq, gk, gv = g_query[...] * SCALE, total[:, :HDIM], total[:, HDIM:]
    m1[...] = row_sums(
        gq * q[...].astype(F32) + gk * kv[:, :HDIM].astype(F32) + gv * kv[:, HDIM:].astype(F32)
    )
    c, s = cos[...], sin[...]

    def back(v):
        return (v * c - pltpu.roll(v, HDIM // 2, 1) * s).astype(BF)

    gq, gk, gv = back(gq), back(gk), gv.astype(BF)
    g_qkv[:, :HDIM] = gq
    g_qkv[:, HDIM : 2 * HDIM] = gk
    g_qkv[:, 2 * HDIM :] = gv
    for k in range(n):
        rows = slice(k * share, (k + 1) * share)
        out[:, rows] = (nt(gq, wq[rows, :]) + nt(gk, wk[rows, :]) + nt(gv, wv[rows, :])).astype(BF)


def call_qkv_back(n, g_query, g_kv, q, kv, cos, sin, wq, wk, wv, arrived):
    n_far = len(arrived)
    tok = q.shape[0]
    bt = min(tok, 256)

    def row(w):
        return pl.BlockSpec((bt, w), lambda i: (i, 0))

    def full(a):
        return pl.BlockSpec(a.shape, lambda i: (0, 0))

    width = wq.shape[0]
    return pl.pallas_call(
        functools.partial(qkv_back_kernel, n, n_far),
        grid=(tok // bt,),
        in_specs=[row(HDIM), row(2 * HDIM), row(HDIM), row(2 * HDIM), row(HDIM), row(HDIM)]
        + [full(a) for a in (wq, wk, wv)]
        + [row(2 * HDIM)] * n_far,
        out_specs=[row(3 * HDIM), pl.BlockSpec((8, bt), lambda i: (0, i)), row(width)],
        out_shape=[shape((tok, 3 * HDIM), BF), shape((8, tok), F32), shape((tok, width), BF)],
        compiler_params=params(),
        cost_estimate=cost(6 * tok * width * 3 * HDIM, 4 * tok * width),
        name="qkv_back",
    )(g_query, g_kv, q, kv, cos, sin, wq, wk, wv, *arrived)


def tail_grad_kernel(n, order, bits, left, g_qkv, mixed, g_hb, *refs):
    outs, parts = refs[:-1], refs[-1]
    share = left.shape[1] // n
    for k in range(n):
        block = slice(k * share, (k + 1) * share)
        value = tn(left[:, block], g_qkv[...]).astype(BF)
        put(parts, bits, order[k] * share, share, slice(0, 3 * HDIM), value)
        value = tn(g_hb[:, block], mixed[...]).astype(BF)
        put(parts, bits, jnp.int32(k * share), share, slice(3 * HDIM, 4 * HDIM), value)
    for i, out in enumerate(outs):
        out[...] = parts[i]


def call_tail_grad(order, bits, left, g_qkv, mixed, g_hb):
    return pl.pallas_call(
        functools.partial(tail_grad_kernel, order.shape[0]),
        out_shape=[shape((left.shape[1] // 4, 4 * HDIM), BF)] * 4,
        in_specs=[SM, SM] + [VM] * 4,
        out_specs=[VM] * 4,
        scratch_shapes=[pltpu.VMEM((4, left.shape[1] // 4, 4 * HDIM), BF)],
        compiler_params=params(),
        cost_estimate=cost(4 * left.shape[0] * left.shape[1] * 4 * HDIM, 4 * left.shape[0] * left.shape[1]),
        name="grad_tail",
    )(order, bits, left, g_qkv, mixed, g_hb)


def folded(n):
    return [0] + list(range(1, n, 2)) + list(range(n - 2 + n % 2, 0, -2))


class Tp:
    def __init__(self, n_tp):
        self.n = n_tp
        self.pairs = n_tp // 2
        ring = folded(self.pairs)
        place = [ring.index(z) for z in range(self.pairs)]
        self.core_perm = [(i, i ^ 1) for i in range(n_tp)]
        self.ring_to = []
        order = []
        for i in range(n_tp):
            z, c = divmod(i, 2)
            self.ring_to.append(ring[(place[z] + 1) % self.pairs] * 2 + c)
            sources = [ring[(place[z] - j) % self.pairs] * 2 for j in range(self.pairs)]
            order.append([s + (c ^ b) for s in sources for b in (0, 1)])
        self.order = jnp.asarray(order, I32)[lax.axis_index("tp")]

    def core(self, a):
        return lax.ppermute(a, "tp", self.core_perm)

    def step(self, a, distance=1):
        perm = []
        for i in range(self.n):
            j = i
            for _ in range(distance):
                j = self.ring_to[j]
            perm.append((i, j))
        return lax.ppermute(a, "tp", perm)

    def gather(self, block, gates=None, beside=None):
        got, cur = [], block
        for j in range(self.pairs):
            if gates and j in gates:
                cur = after(cur, *gates[j](cur))
            if j:
                cur = self.step(cur)
            if beside and j == self.pairs - 1:
                extra = beside(got)
                cur = after(cur, *extra)
            got += [cur, self.core(cur)]
        return (got, extra) if beside else got

    def scatter(self, pieces):
        acc = None
        for j in list(range(1, self.pairs)) + [0]:
            term = pieces[2 * j].astype(F32) + self.core(pieces[2 * j + 1]).astype(F32)
            if acc is not None:
                term = term + self.step(acc.astype(BF)).astype(F32)
            acc = term
        return acc

    def total(self, small):
        small = small + self.core(small)
        return sum([self.step(small, d) for d in range(1, self.pairs)], small)


def scatter_tp(a):
    return lax.psum_scatter(a, "tp", scatter_dimension=1, tiled=True)


def gather_tp(a):
    return lax.all_gather(a, "tp", axis=1, tiled=True)


def after(value, *others):
    return lax.optimization_barrier((value, *others))[0]


class SumCtx:
    def __init__(self, quarters, n_ctx, rank):
        self.n, self.bits = n_ctx, (rank % 2, rank // 2)
        self.quarters = quarters
        self.parts = [None, None] if n_ctx == 4 else [jnp.concatenate(quarters, 0)]
        self.phase = 0
        self.arrived = []

    def send(self):
        if self.n == 4:
            self.arrived = [self.swap(self.quarters[2 * i + 1], i) for i in (0, 1)]
        return self.arrived

    def swap(self, a, axis):
        return lax.ppermute(a, "ctx", [(r, r ^ (1 << axis)) for r in range(4)])

    def run(self, before=(), meanwhile=()):
        phase = self.phase
        self.phase += 1
        parts = [after(p, *before) for p in self.parts] if before else self.parts
        if self.n != 4:
            if phase == 0:
                self.parts = list(lax.psum(tuple(parts), "ctx"))
            return self.parts
        self.parts = []
        self.last = []
        for i, part in enumerate(parts):
            axis = (i + phase) % 2 if phase < 2 else (i + 1 + phase) % 2
            bit = self.bits[axis]
            give = part
            if phase == 0:
                part, give = self.quarters[2 * i : 2 * i + 2]
            elif phase == 1:
                half = part.shape[0] // 2
                give = lax.dynamic_slice_in_dim(part, (1 - bit) * half, half, 0)
                part = lax.dynamic_slice_in_dim(part, bit * half, half, 0)
            got = self.arrived[i] if phase == 0 and self.arrived else self.swap(give, axis)
            if meanwhile:
                got = after(got, *meanwhile)
            self.last.append((bit, part, got))
            if phase < 2:
                self.parts.append((part.astype(F32) + got.astype(F32)).astype(BF))
            elif phase == 2:
                self.parts.append(self.joined(bit, part, got))
        return self.parts or [got for _, _, got in self.last]

    def hold(self, gate):
        if self.n == 4:
            self.last = [(bit, after(part, gate), after(got, gate)) for bit, part, got in self.last]

    def joined(self, bit, part, got):
        return jnp.where(bit == 0, jnp.concatenate([part, got], 0), jnp.concatenate([got, part], 0))

    def result(self, at, first=None, width=None):
        take = slice(None) if first is None else slice(first, first + width)
        if self.n != 4:
            return self.parts[at][:, take].astype(F32)
        both = [self.joined(bit, part[:, take], got[:, take]) for bit, part, got in self.last[2 * at : 2 * at + 2]]
        return jnp.concatenate(both, 0).astype(F32)


def per_device(
    layer_in,
    gain_attn,
    gain_ffn,
    w_query,
    w_key,
    w_value,
    w_out,
    w_gate,
    w_up,
    w_down,
    doc_ids,
    positions,
    cotangent,
):
    tok, share = layer_in.shape
    n_ctx, n_tp = lax.axis_size("ctx"), lax.axis_size("tp")
    width = share * n_tp
    tp = Tp(n_tp)
    order = tp.order
    rank = lax.axis_index("ctx").astype(I32)
    own = lax.axis_index("tp") * share
    bias = -math.log(tok * n_ctx)
    per = max(1, min(4 * HDIM // share, n_tp))
    bits = jnp.stack([rank % 2, rank // 2]) if n_ctx == 4 else jnp.zeros((2,), I32)
    gain_a_own = lax.dynamic_slice_in_dim(gain_attn, own, share, 0)
    gain_f_own = lax.dynamic_slice_in_dim(gain_ffn, own, share, 0)

    def shift(a, s):
        return lax.ppermute(a, "ctx", [(r, r + s) for r in range(n_ctx) if 0 <= r + s < n_ctx])

    def broad(a):
        return jnp.tile(a, (1, share // a.shape[1]))

    freq = THETA ** (-(jnp.arange(HDIM // 2, dtype=F32) * 2.0 / HDIM))
    angle = positions.astype(F32)[:, None] * freq[None, :]
    cos, sin = jnp.cos(angle), jnp.sin(angle)
    cos, sin = jnp.concatenate([cos, cos], 1), jnp.concatenate([-sin, sin], 1)
    q_start = rank * tok + jnp.arange(tok, dtype=I32) - positions
    edges = edges_of(rank, tok, q_start)
    gain_blocks, inv_gain = gain_attn.reshape(n_tp, share), (1.0 / gain_ffn).reshape(n_tp, share)
    start_col, start_row = q_start[:, None], q_start[None, :]
    prepared = lax.optimization_barrier((cos, sin, edges, start_col, start_row, gain_blocks, inv_gain, order))
    cos, sin, edges, start_col, start_row, gain_blocks, inv_gain, order = prepared
    xs = tp.gather(layer_in, {2: lambda arrived: prepared})
    normed, q_rot, kv_own, r1 = call_qkv(order, xs, gain_blocks, w_query, w_key, w_value, cos, sin)
    cot_full = lax.all_gather(after(cotangent, xs[-2]), "tp", axis=1, tiled=True)
    kv_far = [shift(kv_own, s) for s in range(1, n_ctx)]
    acc = call_own(bias, edges, start_col, q_rot, kv_own)
    mixed, *pieces = call_far(bias, tok, 0, tok, edges, order, start_col, q_rot, acc, w_out, kv_far)
    h = layer_in.astype(F32) + tp.scatter(pieces)
    hs, begun = tp.gather(
        (h * gain_f_own).astype(BF),
        beside=lambda got: call_ffn_start(order, got, cot_full, inv_gain, w_gate, w_up, w_down),
    )

    hidden, g_gu, r2, m2, back = call_ffn(order, hs[-2:], begun, inv_gain, w_gate, w_up)
    dn2 = scatter_tp(back)
    m2 = tp.total(m2[0]) / width
    grad_ffn = call_ffn_grad(order, bits, per, cot_full, hs, g_gu, hidden)
    ffn_sum = SumCtx(grad_ffn, n_ctx, rank)
    down = nn(hidden, after(w_down, grad_ffn[1])).astype(BF)
    dn2 = after(dn2, down, *ffn_sum.send()).astype(F32)
    r2 = broad(r2)
    g_h = cotangent.astype(F32) + gain_f_own * dn2 - (r2 * r2 * m2[:, None]) * h
    grad_gain_two = jnp.sum(dn2 * h, axis=0)
    g_h_low = g_h.astype(BF)
    g_hb = gather_tp(g_h_low)
    ffn_sum.run(meanwhile=(g_h_low,))
    ffn_sum.run(meanwhile=(g_h_low,))
    g_hb = after(g_hb, *ffn_sum.run())

    g_mixed = nt(g_hb, w_out).astype(BF)
    g_query, *g_kv_far = call_far_back(bias, edges, start_row, q_rot, g_mixed, kv_far)
    arrived = [shift(g, -s) for s, g in zip(range(1, n_ctx), g_kv_far)]
    g_query, g_kv = call_own_back(bias, edges, start_row, q_rot, g_mixed, kv_own, g_query)
    down = scatter_tp(after(down, g_hb))
    g_kv = after(g_kv, *ffn_sum.run(meanwhile=(g_kv,)))
    g_qkv, m1, back = call_qkv_back(
        n_tp, g_query, g_kv, q_rot, kv_own, cos, sin, w_query, w_key, w_value, arrived
    )
    dn1 = scatter_tp(after(back, down))
    m1 = tp.total(m1[0]) / width
    tail = call_tail_grad(order, bits, normed, g_qkv, mixed, g_hb)
    tail_sum = SumCtx(tail, n_ctx, rank)
    for _ in range(3):
        tail_sum.run()
    hid = w_gate.shape[1]
    ffn_sum.hold(tail[1])
    outs = (h + after(down, tail[1]).astype(F32)).astype(BF)
    down_sum = ffn_sum.result(0, 2 * hid, per * share)
    grad_down = jnp.concatenate([down_sum[i * hid : (i + 1) * hid] for i in range(n_tp // per)], 1)
    grad_gate, grad_up = ffn_sum.result(0, 0, hid), ffn_sum.result(0, hid, hid)
    dn1, outs, grad_gate, grad_up, grad_down = lax.optimization_barrier(
        (dn1, outs, grad_gate, grad_up, grad_down)
    )
    dn1 = dn1.astype(F32)
    r1 = broad(r1)
    x_hat = layer_in.astype(F32) * r1
    g_input = g_h + r1 * (dn1 * gain_a_own - x_hat * m1[:, None])
    grad_gain_one = jnp.sum(dn1 * x_hat, axis=0)
    tail_sum.run(meanwhile=(grad_gain_one,))
    gains = jnp.concatenate([grad_gain_one, grad_gain_two])
    gains = sum(
        [lax.ppermute(gains, "ctx", [(r, (r + s) % n_ctx) for r in range(n_ctx)]) for s in range(1, n_ctx)],
        gains,
    )
    return (
        outs,
        g_input,
        gains[:share],
        gains[share:],
        tail_sum.result(0, 0, HDIM),
        tail_sum.result(0, HDIM, HDIM),
        tail_sum.result(0, 2 * HDIM, HDIM),
        tail_sum.result(0, 3 * HDIM, HDIM).T,
        grad_gate,
        grad_up,
        grad_down,
    )


def solution(mesh):
    row, col = P("tp", None), P(None, "tp")
    both = P("ctx", "tp")
    in_specs = (both, P(), P(), col, col, col, row, col, col, row, P("ctx"), P("ctx"), both)
    out_specs = (both, both, P("tp"), P("tp"), col, col, col, row, col, col, row)
    return jax.shard_map(
        per_device, mesh=mesh, in_specs=in_specs, out_specs=out_specs, check_vma=False
    )
```

```python
import functools
import math

import jax
import jax.numpy as jnp
from jax import lax
from jax.experimental import pallas as pl
from jax.experimental.pallas import tpu as pltpu
from jax.sharding import PartitionSpec as P

HDIM = 128
EPS = 1e-05
THETA = 10000.0
LOG2E = math.log2(math.e)
SCALE = 1.0 / math.sqrt(HDIM)
BF = jnp.bfloat16
F32 = jnp.float32
I32 = jnp.int32
BQ, BK = 512, 512
VMEM_BYTES = 60 * 1024 * 1024
COST = 1.0

SM = pl.BlockSpec(memory_space=pltpu.SMEM)
VM = pl.BlockSpec(memory_space=pltpu.VMEM)


def shape(dims, dtype):
    return jax.ShapeDtypeStruct(dims, dtype)


def params():
    return pltpu.CompilerParams(vmem_limit_bytes=VMEM_BYTES)


def cost(mults, size):
    return pl.CostEstimate(flops=int(2 * mults * COST), bytes_accessed=int(size * COST), transcendentals=0)


def nn(a, b):
    return lax.dot_general(a, b, (((1,), (0,)), ((), ())), preferred_element_type=F32)


def nt(a, b):
    return lax.dot_general(a, b, (((1,), (1,)), ((), ())), preferred_element_type=F32)


def tn(a, b):
    return lax.dot_general(a, b, (((0,), (0,)), ((), ())), preferred_element_type=F32)


def add(a, b):
    return b if a is None else a + b


def tiles(width, k, n=None):
    return pl.ds(pl.multiple_of(k * width, width), width)


def row_sums(a):
    high = a.astype(BF)
    low = (a - high.astype(F32)).astype(BF)
    ones = jnp.ones((8, a.shape[1]), BF)
    return nt(ones, high) + nt(ones, low)


def qkv_kernel(n, order, *refs):
    xs = refs[:n]
    gain, wq, wk, wv, cos, sin, normed, q, kv, r1_out = refs[n:]
    share = xs[0].shape[1]
    squares = None
    for k in range(n):
        v = xs[k][...].astype(F32)
        squares = add(squares, v * v)
    r1 = lax.rsqrt(jnp.sum(squares, axis=-1, keepdims=True) / (n * share) + EPS)
    sums = [None] * 3
    for k in range(n):
        block = (xs[k][...].astype(F32) * r1 * gain[pl.ds(order[k], 1), :]).astype(BF)
        normed[:, k * share : (k + 1) * share] = block
        rows = tiles(share, order[k])
        for i, w in enumerate((wq, wk, wv)):
            sums[i] = add(sums[i], nn(block, w[rows, :]))
    c, s = cos[...], sin[...]

    def rotated(v):
        return v * c + pltpu.roll(v, HDIM // 2, 1) * s

    q[...] = rotated(sums[0]).astype(BF)
    kv[:, :HDIM] = rotated(sums[1]).astype(BF)
    kv[:, HDIM:] = sums[2].astype(BF)
    r1_out[...] = jnp.broadcast_to(r1, r1_out.shape)


def call_qkv(order, xs, gain, wq, wk, wv, cos, sin):
    n = len(xs)
    tok, share = xs[0].shape
    bt = min(tok, 256)

    def row(w):
        return pl.BlockSpec((bt, w), lambda i, o: (i, 0))

    def full(a):
        return pl.BlockSpec(a.shape, lambda i, o: (0, 0))

    spec = pltpu.PrefetchScalarGridSpec(
        num_scalar_prefetch=1,
        grid=(tok // bt,),
        in_specs=[row(share)] * n + [full(a) for a in (gain, wq, wk, wv)] + [row(HDIM)] * 2,
        out_specs=[row(n * share), row(HDIM), row(2 * HDIM), row(128)],
    )
    return pl.pallas_call(
        functools.partial(qkv_kernel, n),
        grid_spec=spec,
        out_shape=[
            shape((tok, n * share), BF),
            shape((tok, HDIM), BF),
            shape((tok, 2 * HDIM), BF),
            shape((tok, 128), F32),
        ],
        compiler_params=params(),
        cost_estimate=cost(5 * tok * n * share * HDIM * 4, 10 * tok * n * share),
        name="norm_qkv",
    )(order, *xs, gain, wq, wk, wv, cos, sin)


def edges_of(rank, tok, starts):
    t = starts.reshape(tok // BQ, BQ)
    return jnp.concatenate([(rank * tok)[None], jnp.stack([t[:, 0], t[:, -1]], axis=1).reshape(-1)])


def sigmoid_of(raw, bias):
    return 1.0 / (1.0 + jnp.exp2(raw * (-LOG2E * SCALE) - bias * LOG2E))


def own_kernel(bias, tok, edges, start, q, kv, total):
    base = edges[0]
    for qi in range(tok // BQ):
        rows = slice(qi * BQ, (qi + 1) * BQ)
        q_tile = q[rows, :]
        first_key = start[rows, :] - base
        q_index = qi * BQ + lax.broadcasted_iota(I32, (BQ, 1), 0)

        def body(ki, acc):
            at = tiles(BK, ki)
            w = sigmoid_of(nt(q_tile, kv[at, :HDIM]), bias)
            k_index = ki * BK + lax.broadcasted_iota(I32, (BQ, BK), 1)
            w = jnp.where((k_index >= first_key) & (k_index <= q_index), w, 0.0)
            return acc + nn(w.astype(BF), kv[at, HDIM:])

        low = jnp.maximum(edges[1 + 2 * qi] - base, 0) // BK
        high = ((qi + 1) * BQ + BK - 1) // BK
        total[rows, :] = lax.fori_loop(low, high, body, jnp.zeros((BQ, HDIM), F32))


def far_kernel(bias, tok, q0, n_far, n, edges, order, start, q, acc, wo, *refs):
    kvs, mixed, pieces = refs[:n_far], refs[n_far], refs[n_far + 1 :]
    share = wo.shape[1] // n
    wide = min(tok, 2 * BK)
    n_keys = tok // wide
    for qi in range(q.shape[0] // BQ):
        rows = slice(qi * BQ, (qi + 1) * BQ)
        at_first, at_last = 1 + 2 * (q0 // BQ + qi), 2 + 2 * (q0 // BQ + qi)
        q_tile = q[rows, :]
        total = acc[rows, :]
        for i in range(n_far):
            base = edges[0] - (i + 1) * tok
            kv = kvs[i]
            first_key = start[rows, :] - base

            def body(ki, total, masked):
                at = tiles(wide, ki)
                w = sigmoid_of(nt(q_tile, kv[at, :HDIM]), bias)
                if masked:
                    k_index = ki * wide + lax.broadcasted_iota(I32, (BQ, wide), 1)
                    w = jnp.where(k_index >= first_key, w, 0.0)
                return total + nn(w.astype(BF), kv[at, HDIM:])

            low = jnp.clip(edges[at_first] - base, 0, tok) // wide
            mid = jnp.clip(edges[at_last] - base + wide - 1, 0, tok) // wide
            mid = jnp.maximum(low, mid)
            total = lax.fori_loop(low, mid, functools.partial(body, masked=True), total)
            total = lax.fori_loop(mid, n_keys, functools.partial(body, masked=False), total)
        rounded = total.astype(BF)
        mixed[rows, :] = rounded
        for k in range(n):
            pieces[k][rows, :] = nn(rounded, wo[:, tiles(share, order[k])]).astype(BF)


def tile_back(bias, q_tile, g_tile, k_tile, v_tile, keep, g_query, rows, sums):
    s = sigmoid_of(nt(k_tile, q_tile), bias)
    g_weight = nt(v_tile, g_tile)
    if keep is not None:
        s = jnp.where(keep, s, 0.0)
    g_s = (g_weight * (s * (1.0 - s))).astype(BF)
    g_value = sums[1] + nn(s.astype(BF), g_tile)
    g_key = sums[0] + nn(g_s, q_tile)
    g_query[rows, :] = g_query[rows, :] + tn(g_s, k_tile)
    return g_key, g_value


def count_tiles(edges, n_q, which, limit):
    return sum([(edges[which + 2 * i] <= limit).astype(I32) for i in range(n_q)], jnp.int32(0))


def far_back_kernel(bias, tok, n_far, edges, start, q, g, *refs):
    kvs, g_query, outs = refs[:n_far], refs[n_far], refs[n_far + 1 :]
    n_q = tok // BQ
    g_query[...] = jnp.zeros_like(g_query)
    for i in reversed(range(n_far)):
        base = edges[0] - (i + 1) * tok
        kv, out = kvs[i], outs[i]

        def key_tile(ki, carry):
            at = tiles(BK, ki)
            k_tile, v_tile = kv[at, :HDIM], kv[at, HDIM:]
            key0 = base + ki * BK
            high = count_tiles(edges, n_q, 1, key0 + BK - 1)
            mid = count_tiles(edges, n_q, 2, key0)

            def body(qi, sums, masked):
                r = tiles(BQ, qi)
                keep = None
                if masked:
                    keep = key0 + lax.broadcasted_iota(I32, (BK, BQ), 0) >= start[:, r]
                return tile_back(bias, q[r, :], g[r, :], k_tile, v_tile, keep, g_query, r, sums)

            zero = jnp.zeros((BK, HDIM), F32)
            sums = lax.fori_loop(0, mid, functools.partial(body, masked=False), (zero, zero))
            g_key, g_value = lax.fori_loop(mid, high, functools.partial(body, masked=True), sums)
            out[at, :HDIM] = (g_key * SCALE).astype(BF)
            out[at, HDIM:] = g_value.astype(BF)
            return carry

        live = jnp.logical_and(base >= 0, edges[1] <= base + tok - 1)

        @pl.when(live)
        def _():
            lax.fori_loop(0, tok // BK, key_tile, 0)

        @pl.when(jnp.logical_not(live))
        def _():
            out[...] = jnp.zeros_like(out)


def own_back_kernel(bias, tok, edges, start, q, g, kv, g_query_in, g_query, out):
    n_q = tok // BQ
    base = edges[0]
    g_query[...] = g_query_in[...]
    for ki in range(tok // BK):
        at = slice(ki * BK, (ki + 1) * BK)
        k_tile, v_tile = kv[at, :HDIM], kv[at, HDIM:]
        key0 = base + ki * BK

        def body(qi, sums):
            r = tiles(BQ, qi)
            k_index = key0 + lax.broadcasted_iota(I32, (BK, BQ), 0)
            q_index = base + qi * BQ + lax.broadcasted_iota(I32, (1, BQ), 1)
            keep = (k_index >= start[:, r]) & (k_index <= q_index)
            return tile_back(bias, q[r, :], g[r, :], k_tile, v_tile, keep, g_query, r, sums)

        zero = jnp.zeros((BK, HDIM), F32)
        high = count_tiles(edges, n_q, 1, key0 + BK - 1)
        g_key, g_value = lax.fori_loop((ki * BK) // BQ, high, body, (zero, zero))
        out[at, :HDIM] = g_key * SCALE
        out[at, HDIM:] = g_value


def call_own(bias, edges, start, q, kv):
    tok = q.shape[0]
    return pl.pallas_call(
        functools.partial(own_kernel, bias, tok),
        out_shape=shape((tok, HDIM), F32),
        in_specs=[SM, VM, VM, VM],
        out_specs=VM,
        compiler_params=params(),
        cost_estimate=cost(16 * tok * tok * HDIM, 4 * tok * HDIM),
        name="attend_own",
    )(edges, start, q, kv)


def call_far(bias, tok, c, rows, edges, order, start, q, acc, wo, kvs):
    n = order.shape[0]

    def part(w):
        return pl.BlockSpec((rows, w), lambda i: (c, 0))

    def full(a):
        return pl.BlockSpec(a.shape, lambda i: (0, 0))

    out = pl.BlockSpec((rows, HDIM), lambda i: (0, 0))
    share = wo.shape[1] // n
    return pl.pallas_call(
        functools.partial(far_kernel, bias, tok, c * rows, len(kvs), n),
        grid=(1,),
        out_shape=[shape((rows, HDIM), BF)] + [shape((rows, share), BF)] * n,
        in_specs=[SM, SM, part(1), part(HDIM), part(HDIM), full(wo)] + [full(a) for a in kvs],
        out_specs=[out] + [pl.BlockSpec((rows, share), lambda i: (0, 0))] * n,
        compiler_params=params(),
        cost_estimate=cost(20 * rows * tok * HDIM + 12 * rows * n * share * HDIM, 4 * rows * n * share),
        name="attend_far",
    )(edges, order, start, q, acc, wo, *kvs)


def call_far_back(bias, edges, start, q, g, kvs):
    tok = q.shape[0]
    return pl.pallas_call(
        functools.partial(far_back_kernel, bias, tok, len(kvs)),
        out_shape=[shape((tok, HDIM), F32)] + [shape((tok, 2 * HDIM), BF)] * len(kvs),
        in_specs=[SM] + [VM] * (3 + len(kvs)),
        out_specs=[VM] * (1 + len(kvs)),
        compiler_params=params(),
        cost_estimate=cost(48 * tok * tok * HDIM, 16 * tok * HDIM),
        name="attend_far_back",
    )(edges, start, q, g, *kvs)


def call_own_back(bias, edges, start, q, g, kv, g_query):
    tok = q.shape[0]
    return pl.pallas_call(
        functools.partial(own_back_kernel, bias, tok),
        out_shape=[shape((tok, HDIM), F32), shape((tok, 2 * HDIM), F32)],
        in_specs=[SM] + [VM] * 5,
        out_specs=[VM] * 2,
        compiler_params=params(),
        cost_estimate=cost(28 * tok * tok * HDIM, 16 * tok * HDIM),
        name="attend_own_back",
    )(edges, start, q, g, kv, g_query)


def ffn_start_kernel(n, order, *refs):
    hs = refs[:n]
    cot, inv_gain, wg, wu, wd, gate_out, up_out, g_hidden, squares_out = refs[n:]
    share = hs[0].shape[1]
    squares = gate = up = None
    for k in range(n):
        h = hs[k][...]
        v = h.astype(F32) * inv_gain[pl.ds(order[k], 1), :]
        squares = add(squares, v * v)
        rows = tiles(share, order[k])
        gate = add(gate, nn(h, wg[rows, :]))
        up = add(up, nn(h, wu[rows, :]))
    gate_out[...] = gate
    up_out[...] = up
    g_hidden[...] = nt(cot[...], wd[...])
    squares_out[...] = squares


def call_ffn_start(order, hs, cot, inv_gain, wg, wu, wd):
    n, (rows, share) = len(hs), hs[0].shape
    hid = wd.shape[0]
    bt = min(rows, 256)

    def row(w):
        return pl.BlockSpec((bt, w), lambda i, o: (i, 0))

    def full(a):
        return pl.BlockSpec(a.shape, lambda i, o: (0, 0))

    spec = pltpu.PrefetchScalarGridSpec(
        num_scalar_prefetch=1,
        grid=(rows // bt,),
        in_specs=[row(share)] * n + [row(cot.shape[1])] + [full(a) for a in (inv_gain, wg, wu, wd)],
        out_specs=[row(hid)] * 3 + [row(share)],
    )
    return pl.pallas_call(
        functools.partial(ffn_start_kernel, n),
        grid_spec=spec,
        out_shape=[shape((rows, hid), F32)] * 3 + [shape((rows, share), F32)],
        compiler_params=params(),
        cost_estimate=cost(2 * 2 * rows * cot.shape[1] * hid, 14 * rows * cot.shape[1]),
        name="ffn_start",
    )(order, *hs, cot, inv_gain, wg, wu, wd)


def ffn_kernel(n, late, order, *refs):
    hs = refs[: len(late)]
    gate, up, g_hidden, squares, inv_gain, wg, wu, hidden, g_gu, r2_out, m2, back = refs[len(late) :]
    share, hid = hs[0].shape[1], wg.shape[1]
    gate, up, squares, g_hidden = gate[...], up[...], squares[...], g_hidden[...]
    for k, h_ref in zip(late, hs):
        h = h_ref[...]
        v = h.astype(F32) * inv_gain[pl.ds(order[k], 1), :]
        squares = squares + v * v
        rows = tiles(share, order[k])
        gate = gate + nn(h, wg[rows, :])
        up = up + nn(h, wu[rows, :])
    r2 = lax.rsqrt(jnp.sum(squares, axis=-1, keepdims=True) / (n * share) + EPS)
    gate = gate * r2
    up = up * r2
    sig = jax.nn.sigmoid(gate)
    silu = gate * sig
    hidden[...] = (silu * up).astype(BF)
    g_gate = g_hidden * up * sig * (1.0 + gate * (1.0 - sig))
    g_up = g_hidden * silu
    m2[...] = row_sums(g_gate * gate + g_up * up)
    g_gate = (g_gate * r2).astype(BF)
    g_up = (g_up * r2).astype(BF)
    g_gu[:, :hid] = g_gate
    g_gu[:, hid:] = g_up
    r2_out[...] = jnp.broadcast_to(r2, r2_out.shape)
    for k in range(n):
        rows = slice(k * share, (k + 1) * share)
        back[:, rows] = (nt(g_gate, wg[rows, :]) + nt(g_up, wu[rows, :])).astype(BF)


def call_ffn(order, hs, begun, inv_gain, wg, wu):
    n = order.shape[0]
    late = list(range(n - len(hs), n))
    rows, share = hs[0].shape
    hid = wg.shape[1]
    bt = min(rows, 256)

    def row(w):
        return pl.BlockSpec((bt, w), lambda i, o: (i, 0))

    def full(a):
        return pl.BlockSpec(a.shape, lambda i, o: (0, 0))

    spec = pltpu.PrefetchScalarGridSpec(
        num_scalar_prefetch=1,
        grid=(rows // bt,),
        in_specs=[row(share)] * len(hs)
        + [row(hid)] * 3
        + [row(share)]
        + [full(a) for a in (inv_gain, wg, wu)],
        out_specs=[row(hid), row(2 * hid), row(128), pl.BlockSpec((8, bt), lambda i, o: (0, i)), row(n * share)],
    )
    return pl.pallas_call(
        functools.partial(ffn_kernel, n, late),
        grid_spec=spec,
        out_shape=[
            shape((rows, hid), BF),
            shape((rows, 2 * hid), BF),
            shape((rows, 128), F32),
            shape((8, rows), F32),
            shape((rows, n * share), BF),
        ],
        compiler_params=params(),
        cost_estimate=cost(2 * 3 * rows * n * share * hid, 14 * rows * n * share),
        name="ffn",
    )(order, *hs, *begun, inv_gain, wg, wu)


def put(parts, bits, row, rows, cols, value):
    size = parts.shape[1]
    quarter = row // size
    half = quarter // 2
    goes = (quarter % 2 != bits[half]).astype(I32)
    at = pl.ds(pl.multiple_of(row - quarter * size, rows), rows)
    parts[half * 2 + goes, at, cols] = value


def ffn_grad_kernel(n, per, order, bits, cot, *refs):
    lefts, g_gu, hidden, outs, parts = refs[:n], refs[n], refs[n + 1], refs[n + 2 : -1], refs[-1]
    share, wide, hid = lefts[0].shape[1], g_gu.shape[1], hidden.shape[1]
    step = min(hid, parts.shape[1])
    for k in range(n):
        value = tn(lefts[k][...], g_gu[...]).astype(BF)
        put(parts, bits, order[k] * share, share, slice(0, wide), value)
        row, col = (k // per) * hid, wide + (k % per) * share
        value = tn(hidden[...], cot[:, k * share : (k + 1) * share]).astype(BF)
        for r in range(0, hid, step):
            put(parts, bits, jnp.int32(row + r), step, slice(col, col + share), value[r : r + step, :])
    for i, out in enumerate(outs):
        out[...] = parts[i]


def call_ffn_grad(order, bits, per, cot, lefts, g_gu, hidden):
    n = order.shape[0]
    wide = g_gu.shape[1] + per * lefts[0].shape[1]
    return pl.pallas_call(
        functools.partial(ffn_grad_kernel, n, per),
        out_shape=[shape((cot.shape[1] // 4, wide), BF)] * 4,
        in_specs=[SM, SM] + [VM] * (3 + len(lefts)),
        out_specs=[VM] * 4,
        scratch_shapes=[pltpu.VMEM((4, cot.shape[1] // 4, wide), BF)],
        compiler_params=params(),
        cost_estimate=cost(2 * cot.shape[0] * cot.shape[1] * wide, 8 * cot.shape[0] * cot.shape[1]),
        name="grad_ffn",
    )(order, bits, cot, *lefts, g_gu, hidden)


def qkv_back_kernel(n, n_far, g_query, g_kv, q, kv, cos, sin, wq, wk, wv, *refs):
    arrived, (g_qkv, m1, out) = refs[:n_far], refs[n_far:]
    share = wq.shape[0] // n
    total = g_kv[...]
    for a in arrived:
        total = total + a[...].astype(F32)
    gq, gk, gv = g_query[...] * SCALE, total[:, :HDIM], total[:, HDIM:]
    m1[...] = row_sums(
        gq * q[...].astype(F32) + gk * kv[:, :HDIM].astype(F32) + gv * kv[:, HDIM:].astype(F32)
    )
    c, s = cos[...], sin[...]

    def back(v):
        return (v * c - pltpu.roll(v, HDIM // 2, 1) * s).astype(BF)

    gq, gk, gv = back(gq), back(gk), gv.astype(BF)
    g_qkv[:, :HDIM] = gq
    g_qkv[:, HDIM : 2 * HDIM] = gk
    g_qkv[:, 2 * HDIM :] = gv
    for k in range(n):
        rows = slice(k * share, (k + 1) * share)
        out[:, rows] = (nt(gq, wq[rows, :]) + nt(gk, wk[rows, :]) + nt(gv, wv[rows, :])).astype(BF)


def call_qkv_back(n, g_query, g_kv, q, kv, cos, sin, wq, wk, wv, arrived):
    n_far = len(arrived)
    tok = q.shape[0]
    bt = min(tok, 256)

    def row(w):
        return pl.BlockSpec((bt, w), lambda i: (i, 0))

    def full(a):
        return pl.BlockSpec(a.shape, lambda i: (0, 0))

    width = wq.shape[0]
    return pl.pallas_call(
        functools.partial(qkv_back_kernel, n, n_far),
        grid=(tok // bt,),
        in_specs=[row(HDIM), row(2 * HDIM), row(HDIM), row(2 * HDIM), row(HDIM), row(HDIM)]
        + [full(a) for a in (wq, wk, wv)]
        + [row(2 * HDIM)] * n_far,
        out_specs=[row(3 * HDIM), pl.BlockSpec((8, bt), lambda i: (0, i)), row(width)],
        out_shape=[shape((tok, 3 * HDIM), BF), shape((8, tok), F32), shape((tok, width), BF)],
        compiler_params=params(),
        cost_estimate=cost(6 * tok * width * 3 * HDIM, 4 * tok * width),
        name="qkv_back",
    )(g_query, g_kv, q, kv, cos, sin, wq, wk, wv, *arrived)


def tail_grad_kernel(n, order, bits, left, g_qkv, mixed, g_hb, *refs):
    outs, parts = refs[:-1], refs[-1]
    share = left.shape[1] // n
    for k in range(n):
        block = slice(k * share, (k + 1) * share)
        value = tn(left[:, block], g_qkv[...]).astype(BF)
        put(parts, bits, order[k] * share, share, slice(0, 3 * HDIM), value)
        value = tn(g_hb[:, block], mixed[...]).astype(BF)
        put(parts, bits, jnp.int32(k * share), share, slice(3 * HDIM, 4 * HDIM), value)
    for i, out in enumerate(outs):
        out[...] = parts[i]


def call_tail_grad(order, bits, left, g_qkv, mixed, g_hb):
    return pl.pallas_call(
        functools.partial(tail_grad_kernel, order.shape[0]),
        out_shape=[shape((left.shape[1] // 4, 4 * HDIM), BF)] * 4,
        in_specs=[SM, SM] + [VM] * 4,
        out_specs=[VM] * 4,
        scratch_shapes=[pltpu.VMEM((4, left.shape[1] // 4, 4 * HDIM), BF)],
        compiler_params=params(),
        cost_estimate=cost(4 * left.shape[0] * left.shape[1] * 4 * HDIM, 4 * left.shape[0] * left.shape[1]),
        name="grad_tail",
    )(order, bits, left, g_qkv, mixed, g_hb)


def folded(n):
    return [0] + list(range(1, n, 2)) + list(range(n - 2 + n % 2, 0, -2))


class Tp:
    def __init__(self, n_tp):
        self.n = n_tp
        self.pairs = n_tp // 2
        ring = folded(self.pairs)
        place = [ring.index(z) for z in range(self.pairs)]
        self.core_perm = [(i, i ^ 1) for i in range(n_tp)]
        self.ring_to = []
        order = []
        for i in range(n_tp):
            z, c = divmod(i, 2)
            self.ring_to.append(ring[(place[z] + 1) % self.pairs] * 2 + c)
            sources = [ring[(place[z] - j) % self.pairs] * 2 for j in range(self.pairs)]
            order.append([s + (c ^ b) for s in sources for b in (0, 1)])
        self.order = jnp.asarray(order, I32)[lax.axis_index("tp")]

    def core(self, a):
        return lax.ppermute(a, "tp", self.core_perm)

    def step(self, a, distance=1):
        perm = []
        for i in range(self.n):
            j = i
            for _ in range(distance):
                j = self.ring_to[j]
            perm.append((i, j))
        return lax.ppermute(a, "tp", perm)

    def gather(self, block, gates=None, beside=None):
        got, cur = [], block
        for j in range(self.pairs):
            if gates and j in gates:
                cur = after(cur, *gates[j](cur))
            if j:
                cur = self.step(cur)
            if beside and j == self.pairs - 1:
                extra = beside(got)
                cur = after(cur, *extra)
            got += [cur, self.core(cur)]
        return (got, extra) if beside else got

    def scatter(self, pieces):
        acc = None
        for j in list(range(1, self.pairs)) + [0]:
            term = pieces[2 * j].astype(F32) + self.core(pieces[2 * j + 1]).astype(F32)
            if acc is not None:
                term = term + self.step(acc.astype(BF)).astype(F32)
            acc = term
        return acc

    def total(self, small):
        small = small + self.core(small)
        return sum([self.step(small, d) for d in range(1, self.pairs)], small)


def scatter_tp(a):
    return lax.psum_scatter(a, "tp", scatter_dimension=1, tiled=True)


def gather_tp(a):
    return lax.all_gather(a, "tp", axis=1, tiled=True)


def after(value, *others):
    return lax.optimization_barrier((value, *others))[0]


class SumCtx:
    def __init__(self, quarters, n_ctx, rank):
        self.n, self.bits = n_ctx, (rank % 2, rank // 2)
        self.quarters = quarters
        self.parts = [None, None] if n_ctx == 4 else [jnp.concatenate(quarters, 0)]
        self.phase = 0
        self.arrived = []

    def send(self):
        if self.n == 4:
            self.arrived = [self.swap(self.quarters[2 * i + 1], i) for i in (0, 1)]
        return self.arrived

    def swap(self, a, axis):
        return lax.ppermute(a, "ctx", [(r, r ^ (1 << axis)) for r in range(4)])

    def run(self, before=(), meanwhile=()):
        phase = self.phase
        self.phase += 1
        parts = [after(p, *before) for p in self.parts] if before else self.parts
        if self.n != 4:
            if phase == 0:
                self.parts = list(lax.psum(tuple(parts), "ctx"))
            return self.parts
        self.parts = []
        self.last = []
        for i, part in enumerate(parts):
            axis = (i + phase) % 2 if phase < 2 else (i + 1 + phase) % 2
            bit = self.bits[axis]
            give = part
            if phase == 0:
                part, give = self.quarters[2 * i : 2 * i + 2]
            elif phase == 1:
                half = part.shape[0] // 2
                give = lax.dynamic_slice_in_dim(part, (1 - bit) * half, half, 0)
                part = lax.dynamic_slice_in_dim(part, bit * half, half, 0)
            got = self.arrived[i] if phase == 0 and self.arrived else self.swap(give, axis)
            if meanwhile:
                got = after(got, *meanwhile)
            self.last.append((bit, part, got))
            if phase < 2:
                self.parts.append((part.astype(F32) + got.astype(F32)).astype(BF))
            elif phase == 2:
                self.parts.append(self.joined(bit, part, got))
        return self.parts or [got for _, _, got in self.last]

    def hold(self, gate):
        if self.n == 4:
            self.last = [(bit, after(part, gate), after(got, gate)) for bit, part, got in self.last]

    def joined(self, bit, part, got):
        return jnp.where(bit == 0, jnp.concatenate([part, got], 0), jnp.concatenate([got, part], 0))

    def result(self, at, first=None, width=None):
        take = slice(None) if first is None else slice(first, first + width)
        if self.n != 4:
            return self.parts[at][:, take].astype(F32)
        both = [self.joined(bit, part[:, take], got[:, take]) for bit, part, got in self.last[2 * at : 2 * at + 2]]
        return jnp.concatenate(both, 0).astype(F32)


def per_device(
    layer_in,
    gain_attn,
    gain_ffn,
    w_query,
    w_key,
    w_value,
    w_out,
    w_gate,
    w_up,
    w_down,
    doc_ids,
    positions,
    cotangent,
):
    tok, share = layer_in.shape
    n_ctx, n_tp = lax.axis_size("ctx"), lax.axis_size("tp")
    width = share * n_tp
    tp = Tp(n_tp)
    order = tp.order
    rank = lax.axis_index("ctx").astype(I32)
    own = lax.axis_index("tp") * share
    bias = -math.log(tok * n_ctx)
    per = max(1, min(4 * HDIM // share, n_tp))
    bits = jnp.stack([rank % 2, rank // 2]) if n_ctx == 4 else jnp.zeros((2,), I32)
    gain_a_own = lax.dynamic_slice_in_dim(gain_attn, own, share, 0)
    gain_f_own = lax.dynamic_slice_in_dim(gain_ffn, own, share, 0)

    def shift(a, s):
        return lax.ppermute(a, "ctx", [(r, r + s) for r in range(n_ctx) if 0 <= r + s < n_ctx])

    def broad(a):
        return jnp.tile(a, (1, share // a.shape[1]))

    freq = THETA ** (-(jnp.arange(HDIM // 2, dtype=F32) * 2.0 / HDIM))
    angle = positions.astype(F32)[:, None] * freq[None, :]
    cos, sin = jnp.cos(angle), jnp.sin(angle)
    cos, sin = jnp.concatenate([cos, cos], 1), jnp.concatenate([-sin, sin], 1)
    q_start = rank * tok + jnp.arange(tok, dtype=I32) - positions
    edges = edges_of(rank, tok, q_start)
    gain_blocks, inv_gain = gain_attn.reshape(n_tp, share), (1.0 / gain_ffn).reshape(n_tp, share)
    start_col, start_row = q_start[:, None], q_start[None, :]
    prepared = lax.optimization_barrier((cos, sin, edges, start_col, start_row, gain_blocks, inv_gain, order))
    cos, sin, edges, start_col, start_row, gain_blocks, inv_gain, order = prepared
    xs = tp.gather(layer_in, {2: lambda arrived: prepared})
    normed, q_rot, kv_own, r1 = call_qkv(order, xs, gain_blocks, w_query, w_key, w_value, cos, sin)
    cot_full = lax.all_gather(after(cotangent, xs[-2]), "tp", axis=1, tiled=True)
    kv_far = [shift(kv_own, s) for s in range(1, n_ctx)]
    acc = call_own(bias, edges, start_col, q_rot, kv_own)
    mixed, *pieces = call_far(bias, tok, 0, tok, edges, order, start_col, q_rot, acc, w_out, kv_far)
    h = layer_in.astype(F32) + tp.scatter(pieces)
    hs, begun = tp.gather(
        (h * gain_f_own).astype(BF),
        beside=lambda got: call_ffn_start(order, got, cot_full, inv_gain, w_gate, w_up, w_down),
    )

    hidden, g_gu, r2, m2, back = call_ffn(order, hs[-2:], begun, inv_gain, w_gate, w_up)
    dn2 = scatter_tp(back)
    m2 = tp.total(m2[0]) / width
    grad_ffn = call_ffn_grad(order, bits, per, cot_full, hs, g_gu, hidden)
    ffn_sum = SumCtx(grad_ffn, n_ctx, rank)
    down = nn(hidden, after(w_down, grad_ffn[1])).astype(BF)
    dn2 = after(dn2, down, *ffn_sum.send()).astype(F32)
    r2 = broad(r2)
    g_h = cotangent.astype(F32) + gain_f_own * dn2 - (r2 * r2 * m2[:, None]) * h
    grad_gain_two = jnp.sum(dn2 * h, axis=0)
    g_h_low = g_h.astype(BF)
    g_hb = gather_tp(g_h_low)
    ffn_sum.run(meanwhile=(g_h_low,))
    ffn_sum.run(meanwhile=(g_h_low,))
    g_hb = after(g_hb, *ffn_sum.run())

    g_mixed = nt(g_hb, w_out).astype(BF)
    g_query, *g_kv_far = call_far_back(bias, edges, start_row, q_rot, g_mixed, kv_far)
    arrived = [shift(g, -s) for s, g in zip(range(1, n_ctx), g_kv_far)]
    g_query, g_kv = call_own_back(bias, edges, start_row, q_rot, g_mixed, kv_own, g_query)
    down = scatter_tp(after(down, g_hb))
    g_kv = after(g_kv, *ffn_sum.run(meanwhile=(g_kv,)))
    g_qkv, m1, back = call_qkv_back(
        n_tp, g_query, g_kv, q_rot, kv_own, cos, sin, w_query, w_key, w_value, arrived
    )
    dn1 = scatter_tp(after(back, down))
    m1 = tp.total(m1[0]) / width
    tail = call_tail_grad(order, bits, normed, g_qkv, mixed, g_hb)
    tail_sum = SumCtx(tail, n_ctx, rank)
    for _ in range(3):
        tail_sum.run()
    hid = w_gate.shape[1]
    ffn_sum.hold(tail[1])
    outs = (h + after(down, tail[1]).astype(F32)).astype(BF)
    down_sum = ffn_sum.result(0, 2 * hid, per * share)
    grad_down = jnp.concatenate([down_sum[i * hid : (i + 1) * hid] for i in range(n_tp // per)], 1)
    grad_gate, grad_up = ffn_sum.result(0, 0, hid), ffn_sum.result(0, hid, hid)
    dn1, outs, grad_gate, grad_up, grad_down = lax.optimization_barrier(
        (dn1, outs, grad_gate, grad_up, grad_down)
    )
    dn1 = dn1.astype(F32)
    r1 = broad(r1)
    x_hat = layer_in.astype(F32) * r1
    g_input = g_h + r1 * (dn1 * gain_a_own - x_hat * m1[:, None])
    grad_gain_one = jnp.sum(dn1 * x_hat, axis=0)
    tail_sum.run(meanwhile=(grad_gain_one,))
    gains = jnp.concatenate([grad_gain_one, grad_gain_two])
    gains = sum(
        [lax.ppermute(gains, "ctx", [(r, (r + s) % n_ctx) for r in range(n_ctx)]) for s in range(1, n_ctx)],
        gains,
    )
    return (
        outs,
        g_input,
        gains[:share],
        gains[share:],
        tail_sum.result(0, 0, HDIM),
        tail_sum.result(0, HDIM, HDIM),
        tail_sum.result(0, 2 * HDIM, HDIM),
        tail_sum.result(0, 3 * HDIM, HDIM).T,
        grad_gate,
        grad_up,
        grad_down,
    )


def solution(mesh):
    row, col = P("tp", None), P(None, "tp")
    both = P("ctx", "tp")
    in_specs = (both, P(), P(), col, col, col, row, col, col, row, P("ctx"), P("ctx"), both)
    out_specs = (both, both, P("tp"), P("tp"), col, col, col, row, col, col, row)
    return jax.shard_map(
        per_device, mesh=mesh, in_specs=in_specs, out_specs=out_specs, check_vma=False
    )
```
